256 devices in a mesh: grp: 8 (over x, core), tile: 32 (over z, y).
Axes of the slice: x: 4, y: 4, z: 8, core: 2. Of those that a mesh axis runs over, the one named last changes fastest.
Arguments:
- fwd_start: float32 [8, 4, 256, 64, 256], P('grp', None, 'tile'), may hold values from -0.2 to 0.2
- adj_start: float32 [8, 4, 256, 64, 256], P('grp', None, 'tile'), may hold values from -6 to 6
- adj_rhs: float32 [8, 4, 256, 64, 256], P('grp', None, 'tile'), may hold values from -6 to 6
- src_cell: int32 [8, 4], P('grp'), may hold values from 0 to 4194303
- group_count: int32 [8], P('grp'), may hold values from 1 to 4, as said below
- region_label: int32 [256, 64, 256], P('tile'), may hold values from 0 to 7
- cut_flag: int32 [256, 64, 256], P('tile'), may hold values 0 or 1
- region_sigma: float32 [8], replicated, may hold values from 0.3 to 3
Outputs:
- gradient: float32 [256, 64, 256], P('tile', 'grp')
The draws below stay inside these ranges and needn't reach their ends.
Inputs may be any that keep to these rules, and one draw needn't show every extreme that they name: `group_count`: some group has all 4 slots live in every draw; which one varies.
All inputs are finite; a program needn't handle non-finite values. No bound on the sum of `cut_flag` on one device may be relied on, other than what follows from the above.
Results may differ from the reference program's by a relative error of at most 0.00021.
Values sent between devices are 32-bit elements; how exact they have to be, the bound alone decides.
No kernel may reach another device: no remote copies, remote signals or barrier semaphores. Data moves between devices by JAX's collectives and lax.ppermute only.
A program may use at most 128 MiB of HBM per device.

```python
import math
import jax
import jax.numpy as jnp
from jax import lax

NY = 64
NZ = 256
SLOTS = 4
REGIONS = 8
ITERS = 2
GROUPS = 8
NX = 256


def draw_group_count(key, part):
    key = jax.random.fold_in(key, 7)
    first, second = jax.random.split(key)
    counts = jax.random.randint(first, (GROUPS,), 1, SLOTS + 1)
    fullest = jax.random.randint(second, (), 0, GROUPS)
    return jnp.where(jnp.arange(GROUPS) == fullest, SLOTS, counts).astype(jnp.int32)


def with_ends(values, rng, low, top_value):
    dims = values.shape
    place = [jax.random.randint(jax.random.fold_in(rng, axis), (), 0, dims[axis]) for axis in range(len(dims))]
    values = values.at[tuple(place)].set(low)
    longest = dims.index(max(dims))
    place[longest] = (place[longest] + 1) % dims[longest]
    return values.at[tuple(place)].set(top_value)


def block_levels(own_key, dims, pieces, least, top_value):
    def one(axis_at, shards_of):
        steps = jax.random.uniform(jax.random.fold_in(jax.random.fold_in(own_key, 6), axis_at), (shards_of,), jnp.float32, least / len(pieces), top_value / len(pieces))
        return jnp.repeat(jnp.exp(steps), dims[axis_at] // shards_of).reshape((-1,) + (1,) * (len(dims) - axis_at - 1))

    level = one(*pieces[0])
    for cut in pieces[1:]:
        level = level * one(*cut)
    return level


def noise(stream_key, extent, width, bound, shards=(), held_as=jnp.bfloat16):
    entries = jax.random.normal(stream_key, extent, jnp.float32) * width
    if len(shards) > 0:
        entries = block_levels(stream_key, extent, shards, -0.22, 0.18) * entries
    return jnp.clip(entries, min=-bound, max=bound).astype(held_as)


def setup_inputs(seed: int = 0) -> dict:
    splits = jax.random.split(jax.random.key(seed), 9)
    fwd_start = jnp.clip(jax.random.uniform(splits[0], (GROUPS, SLOTS, NX, NY, NZ), jnp.float32, -0.2, 0.2) * block_levels(splits[0], (GROUPS, SLOTS, NX, NY, NZ), ((0, 8), (2, 32)), -0.4, 0.0), -0.2, 0.2)
    adj_start = noise(splits[1], (GROUPS, SLOTS, NX, NY, NZ), 1.0, 6.0, ((0, 8), (2, 32)), jnp.float32)
    adj_rhs = noise(splits[2], (GROUPS, SLOTS, NX, NY, NZ), 1.0, 6.0, ((0, 8), (2, 32)), jnp.float32)
    src_cell = with_ends(jax.random.randint(splits[3], (GROUPS, SLOTS), 0, NX * NY * NZ), jax.random.fold_in(splits[3], 1), 0, (NX * NY * NZ) - 1).astype(jnp.int32)
    group_count = draw_group_count(jax.random.fold_in(splits[8], 71), 0)
    region_label = with_ends(jax.random.randint(splits[5], (NX, NY, NZ), 0, REGIONS), jax.random.fold_in(splits[5], 1), 0, REGIONS - 1).astype(jnp.int32)
    cut_flag = with_ends((jax.random.randint(splits[6], (NX, NY, NZ), 0, 4) < 1).astype(jnp.int32), jax.random.fold_in(splits[6], 1), 0, 1)
    region_sigma = jnp.clip(jnp.exp(jax.random.uniform(splits[7], (REGIONS,), jnp.float32, math.log(0.3), math.log(3.0))), 0.3, 3.0)
    return {"fwd_start": fwd_start, "adj_start": adj_start, "adj_rhs": adj_rhs, "src_cell": src_cell, "group_count": group_count, "region_label": region_label, "cut_flag": cut_flag, "region_sigma": region_sigma}


MASS = 0.05
SOURCE_AMP = 64.0


def harmonic(left, right):
    return 2.0 * left * right / (left + right)


def region_conductivity(region_label, region_sigma):
    sigma = jnp.zeros(region_label.shape, jnp.float32)
    for region in range(region_sigma.shape[0]):
        sigma = sigma + jnp.where(region_label == region, region_sigma[region], 0.0)
    return sigma


def lateral_faces(sigma, factor):
    inner_y = harmonic(sigma[:, :-1], sigma[:, 1:]) * factor[:, :-1]
    inner_z = harmonic(sigma[:, :, :-1], sigma[:, :, 1:]) * factor[:, :, :-1]
    face_y = jnp.pad(inner_y, ((0, 0), (1, 1), (0, 0)))
    face_z = jnp.pad(inner_z, ((0, 0), (0, 0), (1, 1)))
    return face_y, face_z


def stencil(field, padded, face_x, face_y, face_z, massive):
    pad_y = jnp.pad(field, ((0, 0), (0, 0), (1, 1), (0, 0)))
    pad_z = jnp.pad(field, ((0, 0), (0, 0), (0, 0), (1, 1)))
    result = massive * field
    result = result + face_x[:-1] * (field - padded[:, :-2]) + face_x[1:] * (field - padded[:, 2:])
    result = result + face_y[:, :-1] * (field - pad_y[:, :, :-2]) + face_y[:, 1:] * (field - pad_y[:, :, 2:])
    result = result + face_z[:, :, :-1] * (field - pad_z[:, :, :, :-2]) + face_z[:, :, 1:] * (field - pad_z[:, :, :, 2:])
    return result


def correlate(forward, adjoint, fwd_next, adj_next, face_x, face_y, face_z, massive, live):
    zero_y = jnp.zeros_like(forward[:, :, :1])
    zero_z = jnp.zeros_like(forward[:, :, :, :1])
    diff_fx = fwd_next - forward
    diff_ax = adj_next - adjoint
    diff_fy = jnp.concatenate([forward[:, :, 1:], zero_y], 2) - forward
    diff_ay = jnp.concatenate([adjoint[:, :, 1:], zero_y], 2) - adjoint
    diff_fz = jnp.concatenate([forward[:, :, :, 1:], zero_z], 3) - forward
    diff_az = jnp.concatenate([adjoint[:, :, :, 1:], zero_z], 3) - adjoint
    corr = face_x[1:] * diff_fx * diff_ax + face_y[:, 1:] * diff_fy * diff_ay
    corr = corr + face_z[:, :, 1:] * diff_fz * diff_az + massive * forward * adjoint
    return jnp.sum(live[:, None, None, None] * corr, axis=0)


def reference(fwd_start, adj_start, adj_rhs, src_cell, group_count, region_label, cut_flag, region_sigma):
    sigma = region_conductivity(region_label, region_sigma)
    factor = 1.0 - 0.5 * cut_flag.astype(jnp.float32)
    sig_pad = jnp.pad(sigma, ((1, 1), (0, 0), (0, 0)))
    fac_pad = jnp.pad(factor, ((1, 1), (0, 0), (0, 0)))
    face_x = harmonic(sig_pad[:-1], sig_pad[1:]) * fac_pad[:-1]
    face_y, face_z = lateral_faces(sigma, factor)
    massive = MASS * sigma
    diag = massive + face_x[:-1] + face_x[1:] + face_y[:, :-1] + face_y[:, 1:] + face_z[:, :, :-1] + face_z[:, :, 1:]
    cells = lax.iota(jnp.int32, NX * NY * NZ)

    def apply(field):
        padded = jnp.pad(field, ((0, 0), (1, 1), (0, 0), (0, 0)))
        return stencil(field, padded, face_x, face_y, face_z, massive)

    def dots(left, right):
        return jnp.sum(left * right, axis=(1, 2, 3))

    total = jnp.zeros((NX, NY, NZ), jnp.float32)
    for group in range(GROUPS):
        source = SOURCE_AMP * (cells[None, :] == src_cell[group][:, None]).astype(jnp.float32)
        rhs = jnp.concatenate([source.reshape(SLOTS, NX, NY, NZ), adj_rhs[group]], 0)
        iterate = jnp.concatenate([fwd_start[group], adj_start[group]], 0)
        resid = rhs - apply(iterate)
        precond = resid / diag
        direction = precond
        rz_now = dots(resid, precond)
        for step in range(ITERS):
            image = apply(direction)
            alpha = (rz_now / dots(direction, image))[:, None, None, None]
            iterate = iterate + alpha * direction
            resid = resid - alpha * image
            precond = resid / diag
            rz_next = dots(resid, precond)
            direction = precond + (rz_next / rz_now)[:, None, None, None] * direction
            rz_now = rz_next
        forward = iterate[:SLOTS]
        adjoint = iterate[SLOTS:]
        zero_x = jnp.zeros_like(forward[:, :1])
        fwd_next = jnp.concatenate([forward[:, 1:], zero_x], 1)
        adj_next = jnp.concatenate([adjoint[:, 1:], zero_x], 1)
        live = (lax.iota(jnp.int32, SLOTS) < group_count[group]).astype(jnp.float32)
        total = total + correlate(forward, adjoint, fwd_next, adj_next, face_x, face_y, face_z, massive, live)
    return -total / SLOTS
```

```python
import functools
import jax
import jax.numpy as jnp
from jax import lax
from jax.experimental import pallas as pl
from jax.experimental.pallas import tpu as pltpu
from jax.sharding import PartitionSpec as P

MASS = 0.05
SOURCE_AMP = 64.0
F32 = jnp.float32
VMEM = pltpu.VMEM
IN_SMEM = pl.BlockSpec(memory_space=pltpu.SMEM)
IN_VMEM = pl.BlockSpec(memory_space=pltpu.VMEM)
IN_HBM = pl.BlockSpec(memory_space=pltpu.HBM)
LIMIT = 24 * 1024 * 1024


def next_y(v):
    return pltpu.roll(v, v.shape[0] - 1, 0)


def prev_y(v):
    return pltpu.roll(v, 1, 0)


def next_z(v):
    return pltpu.roll(v, v.shape[1] - 1, 1)


def prev_z(v):
    return pltpu.roll(v, 1, 1)


def harmonic(left, right):
    return 2.0 * left * right / (left + right)


def harmonic_or_zero(left, right):
    return 2.0 * left * right / jnp.maximum(left + right, 1e-30)


def lateral_faces(sigma, factor, mean):
    rows = lax.broadcasted_iota(jnp.int32, sigma.shape, 0)
    lanes = lax.broadcasted_iota(jnp.int32, sigma.shape, 1)
    face_y = jnp.where(rows < sigma.shape[0] - 1, factor * mean(sigma, next_y(sigma)), 0.0)
    face_z = jnp.where(lanes < sigma.shape[1] - 1, factor * mean(sigma, next_z(sigma)), 0.0)
    return face_y, face_z


def lateral(v, face_y, face_z):
    return face_y * next_y(v) + prev_y(face_y * v) + face_z * next_z(v) + prev_z(face_z * v)


def upper_lateral(v, face_y, face_z):
    return face_y * next_y(v) + face_z * next_z(v)


def folded(v):
    rows, lanes = v.shape
    v = v.reshape(rows // 8, 8, lanes).sum(0)
    total = v[:, :128]
    for at in range(128, lanes, 128):
        total = total + v[:, at : at + 128]
    return total


def plane_source(src, slot, plane, shape):
    rows, lanes = shape
    planes = 8
    cell = src[0, slot] - (lax.axis_index("tile") * planes + plane) * (rows * lanes)
    at = lax.broadcasted_iota(jnp.int32, shape, 0) * lanes + lax.broadcasted_iota(jnp.int32, shape, 1)
    return jnp.where(at == cell, SOURCE_AMP, 0.0).astype(F32)


def edges_kernel(
    table_in, src_in, count, fwd, adj, rhs, label, cut,
    up, down, kxf, ky, kz, dd, inv, mass, weight,
    table, src, lab, flag, sig, fac, xs, rs, sems,
):
    slots = fwd.shape[1]
    planes, rows, lanes = label.shape
    last = planes - 1
    copies = [
        pltpu.make_async_copy(label, lab, sems.at[0]),
        pltpu.make_async_copy(cut, flag, sems.at[1]),
        pltpu.make_async_copy(table_in, table, sems.at[12]),
        pltpu.make_async_copy(src_in, src, sems.at[13]),
        pltpu.make_async_copy(fwd.at[0, :, 0], down.at[pl.ds(0, slots)], sems.at[2]),
        pltpu.make_async_copy(adj.at[0, :, 0], down.at[pl.ds(slots, slots)], sems.at[3]),
        pltpu.make_async_copy(fwd.at[0, :, last], up.at[pl.ds(0, slots)], sems.at[4]),
        pltpu.make_async_copy(adj.at[0, :, last], up.at[pl.ds(slots, slots)], sems.at[5]),
        pltpu.make_async_copy(fwd.at[0, :, pl.ds(1, 2)], xs.at[pl.ds(0, slots), pl.ds(0, 2)], sems.at[6]),
        pltpu.make_async_copy(adj.at[0, :, pl.ds(1, 2)], xs.at[pl.ds(slots, slots), pl.ds(0, 2)], sems.at[7]),
        pltpu.make_async_copy(fwd.at[0, :, last - 1], xs.at[pl.ds(0, slots), 2], sems.at[8]),
        pltpu.make_async_copy(adj.at[0, :, last - 1], xs.at[pl.ds(slots, slots), 2], sems.at[9]),
        pltpu.make_async_copy(rhs.at[0, :, pl.ds(0, 2)], rs.at[:, pl.ds(0, 2)], sems.at[10]),
        pltpu.make_async_copy(rhs.at[0, :, last], rs.at[:, 2], sems.at[11]),
    ]
    for copy in copies:
        copy.start()
    for copy in copies[:4]:
        copy.wait()
    slot = lax.broadcasted_iota(jnp.int32, weight.shape, 0)
    weight[...] = jnp.where(slot < count[0], -1.0 / slots, 0.0).astype(F32)

    @pl.loop(0, planes)
    def _(p):
        names = lab[p]
        value = jnp.full((rows, lanes), table[0], F32)
        for region in range(1, table.shape[0]):
            value = jnp.where(names == region, table[region], value)
        factor = 1.0 - 0.5 * flag[p].astype(F32)
        sig[p] = value
        fac[p] = factor
        mass[p] = MASS * value
        face_y, face_z = lateral_faces(value, factor, harmonic)
        ky[p] = face_y
        kz[p] = face_z

    kxf[0] = jnp.zeros((rows, lanes), F32)
    kxf[planes] = jnp.zeros((rows, lanes), F32)

    @pl.loop(1, planes)
    def _(p):
        kxf[p] = harmonic(sig[p - 1], sig[p]) * fac[p - 1]

    @pl.loop(0, planes)
    def _(p):
        face_y, face_z = ky[p], kz[p]
        diag = mass[p] + kxf[p] + kxf[p + 1] + face_y + prev_y(face_y) + face_z + prev_z(face_z)
        dd[p] = diag
        inv[p] = 1.0 / diag

    for copy in copies[4:]:
        copy.wait()
    up[2 * 2 * slots] = sig[last]
    up[2 * 2 * slots + 1] = fac[last]
    up[2 * 2 * slots + 2] = dd[last]
    down[2 * 2 * slots] = sig[0]
    down[2 * 2 * slots + 1] = fac[0]
    down[2 * 2 * slots + 2] = dd[0]
    systems = 2 * slots
    base = 2 * systems + 3

    def one(s, right):
        x0, x1, x2, x6, x7 = down[s], xs[s, 0], xs[s, 1], xs[s, 2], up[s]
        down[systems + s] = right[0] + lateral(x0, ky[0], kz[0]) + kxf[1] * x1
        up[systems + s] = right[2] + lateral(x7, ky[last], kz[last]) + kxf[last] * x6
        z1 = inv[1] * (right[1] + lateral(x1, ky[1], kz[1]) + kxf[1] * x0 + kxf[2] * x2) - x1
        down[base + s] = kxf[1] * z1

    @pl.loop(0, slots)
    def _(s):
        one(s, [plane_source(src, s, p, (rows, lanes)) for p in (0, 1, last)])

    @pl.loop(0, slots)
    def _(s):
        one(slots + s, [rs[s, 0], rs[s, 1], rs[s, 2]])


def interior_kernel(src_in, fwd, adj, rhs, kxf, ky, kz, dd, inv, x, z, n, moments, src, rs, sems):
    slots = fwd.shape[1]
    planes, rows, lanes = x.shape[1:]
    last = planes - 1
    copies = [
        pltpu.make_async_copy(fwd.at[0], x.at[pl.ds(0, slots)], sems.at[0]),
        pltpu.make_async_copy(adj.at[0], x.at[pl.ds(slots, slots)], sems.at[1]),
        pltpu.make_async_copy(rhs.at[0], rs, sems.at[2]),
        pltpu.make_async_copy(src_in, src, sems.at[3]),
    ]
    for copy in copies:
        copy.start()
    for copy in copies:
        copy.wait()

    def one(s, right):
        for p in range(1, last):
            total = right(p) + lateral(x[s, p], ky[p], kz[p])
            total = total + kxf[p] * x[s, p - 1] + kxf[p + 1] * x[s, p + 1]
            z[s, p] = inv[p] * total - x[s, p]
        c0 = jnp.zeros((8, 128), F32)
        c1, c2, c3 = c0, c0, c0
        for p in range(1, last):
            v = z[s, p]
            c0 = c0 + folded(dd[p] * v * v)
            w = lateral(v, ky[p], kz[p])
            if p > 1:
                w = w + kxf[p] * z[s, p - 1]
            if p < last - 1:
                w = w + kxf[p + 1] * z[s, p + 1]
            if p == 1 or p == last - 1:
                n[s, p] = w
                continue
            m = inv[p] * w
            n[s, p] = m
            c1 = c1 + folded(v * w)
            c2 = c2 + folded(m * w)
            near = upper_lateral(m, ky[p], kz[p])
            if p > 2:
                near = near + kxf[p] * n[s, p - 1]
            c3 = c3 + folded(m * near)
        for at, c in enumerate((c0, c1, c2, c3)):
            moments[s, at] = c

    @pl.loop(0, slots)
    def _(s):
        one(s, lambda p: plane_source(src, s, p, (rows, lanes)))

    @pl.loop(0, slots)
    def _(s):
        one(slots + s, lambda p: rs[s, p])


def boundary_kernel(
    below, above, up, down, kxf, ky, kz, dd, inv, z_in, n_in, moments,
    z, n, zx, nx, kch, out,
    coef, sums,
):
    systems, planes, rows, lanes = z.shape
    last = planes - 1
    base = 2 * systems + 3
    sig, fac, deg = 2 * systems, 2 * systems + 1, 2 * systems + 2
    low = harmonic(below[sig], down[sig]) * below[fac]
    high = harmonic(up[sig], above[sig]) * up[fac]
    kch[...] = high
    coef[0] = low
    d0 = dd[0] + low
    d7 = dd[last] + high
    dm = below[deg] + low
    d8 = above[deg] + high
    coef[1] = d0
    coef[2] = d7
    coef[3] = 1.0 / d0
    coef[4] = 1.0 / d7
    coef[5] = jnp.where(dm > 0.0, 1.0 / jnp.where(dm > 0.0, dm, 1.0), 0.0)
    coef[6] = jnp.where(d8 > 0.0, 1.0 / jnp.where(d8 > 0.0, d8, 1.0), 0.0)
    face_y, face_z = lateral_faces(above[sig], above[fac], harmonic_or_zero)
    coef[7] = face_y
    coef[8] = face_z

    @pl.loop(0, systems)
    def _(s):
        c0, c1, c2, c3 = [moments[s, at] for at in range(4)]
        kc, i0, i1 = coef[0], coef[3], inv[1]
        x0, xm = down[s], below[s]
        z0 = i0 * (down[systems + s] + kc * xm) - x0
        zm = coef[5] * (below[systems + s] + kc * x0) - xm
        z1 = z_in[s, 1]
        w0 = lateral(z0, ky[0], kz[0]) + kxf[1] * z1 + kc * zm
        w1 = n_in[s, 1] + kxf[1] * z0
        n0 = i0 * w0
        n1 = i1 * w1
        z[s, 0] = z0
        n[s, 0] = n0
        n[s, 1] = n1
        c0 = c0 + folded(coef[1] * z0 * z0)
        c1 = c1 + folded(z0 * w0 + z1 * w1)
        c2 = c2 + folded(n0 * w0 + n1 * w1)
        near0 = upper_lateral(n0, ky[0], kz[0]) + kxf[1] * n1
        near1 = upper_lateral(n1, ky[1], kz[1]) + kxf[2] * n_in[s, 2]
        c3 = c3 + folded(n0 * near0 + n1 * near1)
        kc, i7, i6 = kch[...], coef[4], inv[last - 1]
        x7, x8 = up[s], above[s]
        z7 = i7 * (up[systems + s] + kc * x8) - x7
        z8 = coef[6] * (above[systems + s] + kc * x7) - x8
        z6 = z_in[s, last - 1]
        w7 = lateral(z7, ky[last], kz[last]) + kxf[last] * z6 + kc * z8
        w6 = n_in[s, last - 1] + kxf[last] * z7
        w8 = lateral(z8, coef[7], coef[8]) + above[base + s] + kc * z7
        n7 = i7 * w7
        n6 = i6 * w6
        n8 = coef[6] * w8
        z[s, last] = z7
        n[s, last] = n7
        n[s, last - 1] = n6
        zx[s] = z8
        nx[s] = n8
        c0 = c0 + folded(coef[2] * z7 * z7)
        c1 = c1 + folded(z7 * w7 + z6 * w6)
        c2 = c2 + folded(n7 * w7 + n6 * w6)
        near7 = upper_lateral(n7, ky[last], kz[last]) + kc * n8
        near6 = upper_lateral(n6, ky[last - 1], kz[last - 1]) + kxf[last] * n7
        near6 = near6 + kxf[last - 1] * n_in[s, last - 2]
        c3 = c3 + folded(n7 * near7 + n6 * near6)
        for at, c in enumerate((c0, c1, c2, c3 + c3)):
            sums[at, pl.ds(s, 1)] = c.sum(0, keepdims=True)

    lanes_at = lax.broadcasted_iota(jnp.int32, (systems, 128), 1)
    packed = jnp.zeros((systems, 128), F32)
    for at in range(4):
        packed = packed + jnp.where(lanes_at == at, sums[at].sum(1, keepdims=True), 0.0)
    out[...] = jnp.broadcast_to(packed[None], out.shape)


def correlate_kernel(weight, parts, x, z, n, above, zx, nx, kxf, kch, ky, kz, mass, out, scale):
    systems, planes, rows, lanes = z.shape
    slots = systems // 2
    last = planes - 1
    total = parts[...].sum(0)
    lanes_at = lax.broadcasted_iota(jnp.int32, total.shape, 1)
    c0, c1, c2, c3 = [
        jnp.where(lanes_at == at, total, 0.0).sum(1, keepdims=True) for at in range(4)
    ]
    alpha = c0 / (c0 - c1)
    keep = 1.0 - alpha
    rz = keep * keep * c0 + 2.0 * alpha * keep * c1 + alpha * alpha * c2
    first = keep + rz / c0
    curve = first * first * (c0 - c1) + 2.0 * first * alpha * (c1 - c2) + alpha * alpha * (c2 - c3)
    step = rz / curve
    scale[0] = jnp.broadcast_to(alpha + step * first, (systems, lanes))
    scale[1] = jnp.broadcast_to(step * alpha, (systems, lanes))
    out[...] = jnp.zeros(out.shape, F32)

    @pl.loop(0, slots)
    def _(s):
        ends = (s, slots + s)
        share = weight[pl.ds(s, 1)]
        on_z = [scale[0, pl.ds(e, 1)] for e in ends]
        on_n = [scale[1, pl.ds(e, 1)] for e in ends]

        def field(p):
            if p < planes:
                return [x[e, p] + on_z[i] * z[e, p] + on_n[i] * n[e, p] for i, e in enumerate(ends)]
            return [above[e] + on_z[i] * zx[e] + on_n[i] * nx[e] for i, e in enumerate(ends)]

        u, v = field(0)
        for p in range(planes):
            u_up, v_up = field(p + 1)
            face_x = kxf[p + 1] if p < last else kch[...]
            corr = face_x * (u_up - u) * (v_up - v)
            corr = corr + ky[p] * (next_y(u) - u) * (next_y(v) - v)
            corr = corr + kz[p] * (next_z(u) - u) * (next_z(v) - v)
            corr = corr + mass[p] * u * v
            out[:, p] = out[:, p] + (share * corr).reshape(out.shape[0], -1, lanes)
            u, v = u_up, v_up


def local(
    fwd_start, adj_start, adj_rhs, src_cell, group_count, region_label, cut_flag, region_sigma
):
    slots = fwd_start.shape[1]
    systems = 2 * slots
    planes, rows, lanes = region_label.shape
    groups = lax.axis_size("grp")
    tiles = lax.axis_size("tile")
    cells = planes * rows * lanes

    def held(*shape):
        return VMEM(shape, F32)

    def in_hbm(*arrays):
        return [pltpu.with_memory_space_constraint(a, pltpu.HBM) for a in arrays]

    def pinned(*arrays):
        return [pltpu.with_memory_space_constraint(a, pltpu.VMEM) for a in arrays]

    def params(**more):
        return pltpu.CompilerParams(vmem_limit_bytes=LIMIT, **more)

    field = held(systems, planes, rows, lanes)
    plane_set = held(planes, rows, lanes)
    up, down, kxf, ky, kz, dd, inv, mass, weight = pl.pallas_call(
        edges_kernel,
        out_shape=[
            held(2 * systems + 3, rows, lanes),
            held(3 * systems + 3, rows, lanes),
            held(planes + 1, rows, lanes),
            plane_set, plane_set, plane_set, plane_set, plane_set,
            held(8, lanes),
        ],
        in_specs=[IN_HBM] * 2 + [IN_SMEM] + [IN_HBM] * 5,
        out_specs=[IN_VMEM] * 9,
        scratch_shapes=[
            pltpu.SMEM(region_sigma.shape, F32),
            pltpu.SMEM(src_cell.shape, jnp.int32),
            VMEM((planes, rows, lanes), jnp.int32),
            VMEM((planes, rows, lanes), jnp.int32),
            VMEM((planes, rows, lanes), F32),
            VMEM((planes, rows, lanes), F32),
            VMEM((systems, 3, rows, lanes), F32),
            VMEM((slots, 3, rows, lanes), F32),
            pltpu.SemaphoreType.DMA((14,)),
        ],
        compiler_params=params(),
        cost_estimate=pl.CostEstimate(flops=20 * cells, bytes_accessed=16 * cells, transcendentals=0),
        name="edges",
    )(
        *in_hbm(region_sigma, src_cell), group_count,
        *in_hbm(fwd_start, adj_start, adj_rhs, region_label, cut_flag),
    )

    below = lax.ppermute(up, "tile", [(i, i + 1) for i in range(tiles - 1)])
    above = lax.ppermute(down, "tile", [(i + 1, i) for i in range(tiles - 1)])

    x, z, n, moments = pl.pallas_call(
        interior_kernel,
        out_shape=[field, field, field, held(systems, 4, 8, 128)],
        in_specs=[IN_HBM] * 4 + [IN_VMEM] * 5,
        out_specs=[IN_VMEM] * 4,
        scratch_shapes=[
            pltpu.SMEM(src_cell.shape, jnp.int32),
            VMEM((slots, planes, rows, lanes), F32),
            pltpu.SemaphoreType.DMA((4,)),
        ],
        compiler_params=params(),
        cost_estimate=pl.CostEstimate(
            flops=60 * systems * cells, bytes_accessed=32 * systems * cells, transcendentals=0
        ),
        name="interior",
    )(*in_hbm(src_cell, fwd_start, adj_start, adj_rhs), *pinned(kxf, ky, kz, dd, inv))

    z, n, zx, nx, kch, moments = pl.pallas_call(
        boundary_kernel,
        out_shape=[
            field, field,
            held(systems, rows, lanes), held(systems, rows, lanes), held(rows, lanes),
            held(tiles, systems, 128),
        ],
        in_specs=[IN_VMEM] * 12,
        out_specs=[IN_VMEM] * 6,
        input_output_aliases={9: 0, 10: 1},
        scratch_shapes=[
            VMEM((9, rows, lanes), F32),
            VMEM((4, systems, 128), F32),
        ],
        compiler_params=params(),
        name="boundary",
    )(*pinned(below, above, up, down, kxf, ky, kz, dd, inv, z, n, moments))

    parts = lax.all_to_all(moments, "tile", 0, 0)

    term = pl.pallas_call(
        correlate_kernel,
        out_shape=held(groups, planes, rows // groups, lanes),
        in_specs=[IN_VMEM] * 13,
        out_specs=IN_VMEM,
        scratch_shapes=[VMEM((2, systems, lanes), F32)],
        compiler_params=params(),
        name="correlate",
    )(*pinned(weight, parts, x, z, n, above, zx, nx, kxf, kch, ky, kz, mass))

    blocks = lax.all_to_all(term, "grp", 0, 0)
    return jnp.sum(blocks, axis=0)


def solution(mesh):
    in_specs = (
        P("grp", None, "tile", None, None),
        P("grp", None, "tile", None, None),
        P("grp", None, "tile", None, None),
        P("grp", None),
        P("grp"),
        P("tile", None, None),
        P("tile", None, None),
        P(),
    )
    out_specs = P("tile", "grp", None)
    return jax.shard_map(local, mesh=mesh, in_specs=in_specs, out_specs=out_specs, check_vma=False)
```

```python
import functools
import jax
import jax.numpy as jnp
from jax import lax
from jax.experimental import pallas as pl
from jax.experimental.pallas import tpu as pltpu
from jax.sharding import PartitionSpec as P

MASS = 0.05
SOURCE_AMP = 64.0
F32 = jnp.float32
VMEM = pltpu.VMEM
IN_SMEM = pl.BlockSpec(memory_space=pltpu.SMEM)
IN_VMEM = pl.BlockSpec(memory_space=pltpu.VMEM)
IN_HBM = pl.BlockSpec(memory_space=pltpu.HBM)
LIMIT = 24 * 1024 * 1024


def next_y(v):
    return pltpu.roll(v, v.shape[0] - 1, 0)


def prev_y(v):
    return pltpu.roll(v, 1, 0)


def next_z(v):
    return pltpu.roll(v, v.shape[1] - 1, 1)


def prev_z(v):
    return pltpu.roll(v, 1, 1)


def harmonic(left, right):
    return 2.0 * left * right / (left + right)


def harmonic_or_zero(left, right):
    return 2.0 * left * right / jnp.maximum(left + right, 1e-30)


def lateral_faces(sigma, factor, mean):
    rows = lax.broadcasted_iota(jnp.int32, sigma.shape, 0)
    lanes = lax.broadcasted_iota(jnp.int32, sigma.shape, 1)
    face_y = jnp.where(rows < sigma.shape[0] - 1, factor * mean(sigma, next_y(sigma)), 0.0)
    face_z = jnp.where(lanes < sigma.shape[1] - 1, factor * mean(sigma, next_z(sigma)), 0.0)
    return face_y, face_z


def lateral(v, face_y, face_z):
    return face_y * next_y(v) + prev_y(face_y * v) + face_z * next_z(v) + prev_z(face_z * v)


def upper_lateral(v, face_y, face_z):
    return face_y * next_y(v) + face_z * next_z(v)


def folded(v):
    rows, lanes = v.shape
    v = v.reshape(rows // 8, 8, lanes).sum(0)
    total = v[:, :128]
    for at in range(128, lanes, 128):
        total = total + v[:, at : at + 128]
    return total


def plane_source(src, slot, plane, shape):
    rows, lanes = shape
    planes = 8
    cell = src[0, slot] - (lax.axis_index("tile") * planes + plane) * (rows * lanes)
    at = lax.broadcasted_iota(jnp.int32, shape, 0) * lanes + lax.broadcasted_iota(jnp.int32, shape, 1)
    return jnp.where(at == cell, SOURCE_AMP, 0.0).astype(F32)


def head_kernel(
    table_in, count, fwd, adj, label, cut,
    msg_a, msg_b, kxf, ky, kz, dd, inv, mass, weight,
    table, lab, flag, sig, fac, sems,
):
    slots = fwd.shape[1]
    planes, rows, lanes = label.shape
    last = planes - 1
    systems = 2 * slots
    core = lax.rem(lax.axis_index("grp"), 2)
    copies = [
        pltpu.make_async_copy(label, lab, sems.at[0]),
        pltpu.make_async_copy(cut, flag, sems.at[1]),
        pltpu.make_async_copy(table_in, table, sems.at[2]),
    ]
    edges = [(msg_a, jnp.where(core == 0, last, 0)), (msg_b, jnp.where(core == 1, last, 0))]
    for at, (msg, edge) in enumerate(edges):
        for half, source in enumerate((fwd, adj)):
            copies.append(
                pltpu.make_async_copy(
                    source.at[0, :, edge], msg.at[pl.ds(half * slots, slots)], sems.at[3 + 2 * at + half]
                )
            )
    for copy in copies:
        copy.start()
    slot = lax.broadcasted_iota(jnp.int32, weight.shape, 0)
    weight[...] = jnp.where(slot < count[0], -1.0 / slots, 0.0).astype(F32)
    for copy in copies[:3]:
        copy.wait()

    @pl.loop(0, planes)
    def _(p):
        names = lab[p]
        value = jnp.full((rows, lanes), table[0], F32)
        for region in range(1, table.shape[0]):
            value = jnp.where(names == region, table[region], value)
        factor = 1.0 - 0.5 * flag[p].astype(F32)
        sig[p] = value
        fac[p] = factor
        mass[p] = MASS * value
        face_y, face_z = lateral_faces(value, factor, harmonic)
        ky[p] = face_y
        kz[p] = face_z

    kxf[0] = jnp.zeros((rows, lanes), F32)
    kxf[planes] = jnp.zeros((rows, lanes), F32)

    @pl.loop(1, planes)
    def _(p):
        kxf[p] = harmonic(sig[p - 1], sig[p]) * fac[p - 1]

    @pl.loop(0, planes)
    def _(p):
        face_y, face_z = ky[p], kz[p]
        diag = mass[p] + kxf[p] + kxf[p + 1] + face_y + prev_y(face_y) + face_z + prev_z(face_z)
        dd[p] = diag
        inv[p] = 1.0 / diag

    for msg, edge in edges:
        msg[systems] = sig[edge]
        msg[systems + 1] = fac[edge]
        msg[systems + 2] = dd[edge]
    for copy in copies[3:]:
        copy.wait()


def edges_kernel(
    src_in, fwd, adj, rhs, head_a, head_b, kxf, ky, kz, inv, msg_a, msg_b, src, xs, rs, sems
):
    slots = fwd.shape[1]
    systems = 2 * slots
    planes, rows, lanes = ky.shape
    last = planes - 1
    first, other = pl.ds(0, slots), pl.ds(slots, slots)
    copies = [
        pltpu.make_async_copy(src_in, src, sems.at[0]),
        pltpu.make_async_copy(fwd.at[0, :, pl.ds(1, 2)], xs.at[first, pl.ds(0, 2)], sems.at[1]),
        pltpu.make_async_copy(adj.at[0, :, pl.ds(1, 2)], xs.at[other, pl.ds(0, 2)], sems.at[2]),
        pltpu.make_async_copy(fwd.at[0, :, pl.ds(planes - 3, 2)], xs.at[first, pl.ds(2, 2)], sems.at[3]),
        pltpu.make_async_copy(adj.at[0, :, pl.ds(planes - 3, 2)], xs.at[other, pl.ds(2, 2)], sems.at[4]),
        pltpu.make_async_copy(rhs.at[0, :, pl.ds(0, 2)], rs.at[:, pl.ds(0, 2)], sems.at[5]),
        pltpu.make_async_copy(rhs.at[0, :, pl.ds(planes - 2, 2)], rs.at[:, pl.ds(2, 2)], sems.at[6]),
    ]
    for copy in copies:
        copy.start()
    for copy in copies:
        copy.wait()
    core = lax.rem(lax.axis_index("grp"), 2)
    half = slots // 2
    for head, msg, up in ((head_a, msg_a, core == 0), (head_b, msg_b, core == 1)):
        edge, inner = jnp.where(up, last, 0), jnp.where(up, last - 1, 1)
        at_inner, at_next = jnp.where(up, 3, 0), jnp.where(up, 2, 1)
        rs_edge, rs_inner = jnp.where(up, 3, 0), jnp.where(up, 2, 1)
        face, face_next = jnp.where(up, last, 1), jnp.where(up, last - 1, 2)
        lead = jnp.where(up, half, 0)

        def partial(s, right):
            msg[s] = right + lateral(head[s], ky[edge], kz[edge]) + kxf[face] * xs[s, at_inner]

        def onward(at, s, right):
            x1 = xs[s, at_inner]
            total = right + lateral(x1, ky[inner], kz[inner])
            total = total + kxf[face] * head[s] + kxf[face_next] * xs[s, at_next]
            msg[systems + at] = kxf[face] * (inv[inner] * total - x1)

        @pl.loop(0, slots)
        def _(s):
            partial(s, plane_source(src, s, edge, (rows, lanes)))
            partial(slots + s, rs[s, rs_edge])

        @pl.loop(0, half)
        def _(s):
            slot = lead + s
            onward(s, slot, plane_source(src, slot, inner, (rows, lanes)))
            onward(half + s, slots + slot, rs[slot, rs_inner])


def interior_kernel(src_in, fwd, adj, rhs, kxf, ky, kz, dd, inv, x, z, n, moments, extra, src, rs, sems):
    slots = fwd.shape[1]
    planes, rows, lanes = x.shape[1:]
    last = planes - 1
    copies = [
        pltpu.make_async_copy(fwd.at[0], x.at[pl.ds(0, slots)], sems.at[0]),
        pltpu.make_async_copy(adj.at[0], x.at[pl.ds(slots, slots)], sems.at[1]),
        pltpu.make_async_copy(rhs.at[0], rs, sems.at[2]),
        pltpu.make_async_copy(src_in, src, sems.at[3]),
    ]
    for copy in copies:
        copy.start()
    for copy in copies:
        copy.wait()

    def one(s, right):
        for p in range(1, last):
            total = right(p) + lateral(x[s, p], ky[p], kz[p])
            total = total + kxf[p] * x[s, p - 1] + kxf[p + 1] * x[s, p + 1]
            z[s, p] = inv[p] * total - x[s, p]
        c0 = jnp.zeros((8, 128), F32)
        c1, c2, c3 = c0, c0, c0
        for p in range(1, last):
            v = z[s, p]
            c0 = c0 + folded(dd[p] * v * v)
            w = lateral(v, ky[p], kz[p])
            if p > 1:
                w = w + kxf[p] * z[s, p - 1]
            if p < last - 1:
                w = w + kxf[p + 1] * z[s, p + 1]
            if p == 1 or p == last - 1:
                n[s, p] = w
                continue
            m = inv[p] * w
            n[s, p] = m
            c1 = c1 + folded(v * w)
            c2 = c2 + folded(m * w)
            near = upper_lateral(m, ky[p], kz[p])
            if p > 2:
                near = near + kxf[p] * n[s, p - 1]
            c3 = c3 + folded(m * near)
        for at, c in enumerate((c0, c1, c2, c3)):
            moments[s, at] = c

    @pl.loop(0, slots)
    def _(s):
        one(s, lambda p: plane_source(src, s, p, (rows, lanes)))

    @pl.loop(0, slots)
    def _(s):
        one(slots + s, lambda p: rs[s, p])

    half = slots // 2
    for at in range(half):
        extra[at] = kxf[1] * z[half + at, 1]
        extra[half + at] = kxf[1] * z[slots + half + at, 1]


def both_sides(planes, slots, pairs):
    last, half = planes - 1, slots // 2
    core = lax.rem(lax.axis_index("grp"), 2)
    found = []
    for at, pair in enumerate(pairs):
        low = core == at
        found.append(
            (
                at, pair, low, jnp.where(low, 0, 1),
                jnp.where(low, 0, last), jnp.where(low, 1, last - 1), jnp.where(low, 2, last - 2),
                jnp.where(low, 1, last), jnp.where(low, 2, last - 1), jnp.where(low, half, 0),
            )
        )
    return found


def near_kernel(
    got_a, got_b, head_a, head_b, msg_a, msg_b, kxf, ky, kz, dd, inv, z_in, n_in, moments_in,
    z, n, part, ext_x, far, moments,
    coef,
):
    systems, planes, rows, lanes = z.shape
    sides = both_sides(planes, systems // 2, ((got_a, head_b, msg_b), (got_b, head_a, msg_a)))
    for at, (got, head, _), low, side, edge, _, _, _, _, _ in sides:
        cross = harmonic(got[systems], head[systems])
        cross = cross * jnp.where(low, got[systems + 1], head[systems + 1])
        here = dd[edge] + cross
        there = got[systems + 2] + cross
        real = there > 0.0
        coef[at] = here
        far[side, 0] = cross
        far[side, 1] = jnp.where(real, 1.0 / jnp.where(real, there, 1.0), 0.0)
        face_y, face_z = lateral_faces(got[systems], got[systems + 1], harmonic_or_zero)
        far[side, 2] = face_y
        far[side, 3] = face_z
        far[side, 4] = 1.0 / here

    @pl.loop(0, systems)
    def _(s):
        c0, c1, c2, c3 = [moments_in[s, at] for at in range(4)]
        for at, (got, head, msg), _, side, edge, inner, third, face, face_next, _ in sides:
            xm = got[s]
            z0 = far[side, 4] * (msg[s] + far[side, 0] * xm) - head[s]
            z1 = z_in[s, inner]
            w0 = lateral(z0, ky[edge], kz[edge]) + kxf[face] * z1
            w1 = n_in[s, inner] + kxf[face] * z0
            n1 = inv[inner] * w1
            z[s, edge] = z0
            n[s, inner] = n1
            part[side, s] = w0
            ext_x[side, s] = xm
            c0 = c0 + folded(coef[at] * z0 * z0)
            c1 = c1 + folded(z0 * w0 + z1 * w1)
            c2 = c2 + folded(n1 * w1)
            near1 = upper_lateral(n1, ky[inner], kz[inner]) + kxf[face_next] * n_in[s, third]
            c3 = c3 + folded(n1 * near1)
        for at, c in enumerate((c0, c1, c2, c3)):
            moments[s, at] = c


def boundary_kernel(
    got_a, got_b, head_a, head_b, kxf, ky, kz, far, ext_x, part, z, n_in, moments,
    n, ext_z, ext_n, out,
    sums,
):
    systems, planes, rows, lanes = n.shape
    slots = systems // 2
    half = slots // 2
    sides = both_sides(planes, slots, ((got_a, head_b), (got_b, head_a)))

    @pl.loop(0, systems)
    def _(s):
        c0, c1, c2, c3 = [moments[s, at] for at in range(4)]
        for _, (got, head), _, side, edge, inner, _, face, _, _ in sides:
            cross = far[side, 0]
            z0 = z[s, edge]
            zm = far[side, 1] * (got[s] + cross * head[s]) - ext_x[side, s]
            over = cross * zm
            w0 = part[side, s] + over
            n0 = far[side, 4] * w0
            n[s, edge] = n0
            ext_z[side, s] = zm
            c1 = c1 + folded(z0 * over)
            c2 = c2 + folded(n0 * w0)
            near0 = upper_lateral(n0, ky[edge], kz[edge]) + kxf[face] * n_in[s, inner]
            c3 = c3 + folded(n0 * near0)
        for at, c in enumerate((c0, c1, c2, c3 + c3)):
            sums[at, pl.ds(s, 1)] = c.sum(0, keepdims=True)

    @pl.loop(0, half)
    def _(at):
        for _, (got, _), _, side, edge, _, _, _, _, lead in sides:
            for place, s in ((at, lead + at), (half + at, slots + lead + at)):
                cross = far[side, 0]
                w = lateral(ext_z[side, s], far[side, 2], far[side, 3])
                w = w + got[systems + place] + cross * z[s, edge]
                nm = far[side, 1] * w
                ext_n[side, s] = nm
                pair = folded(cross * nm * n[s, edge])
                sums[3, pl.ds(s, 1)] = sums[3, pl.ds(s, 1)] + 2.0 * pair.sum(0, keepdims=True)

    lanes_at = lax.broadcasted_iota(jnp.int32, (systems, 128), 1)
    packed = jnp.zeros((systems, 128), F32)
    for at in range(4):
        packed = packed + jnp.where(lanes_at == at, sums[at].sum(1, keepdims=True), 0.0)
    out[...] = jnp.broadcast_to(packed[None], out.shape)


def correlate_kernel(
    weight, parts, x, z, n, ext_x, ext_z, ext_n, far, extra, kxf, ky, kz, mass, keep, give, scale, total
):
    systems, planes, rows, lanes = z.shape
    slots = systems // 2
    half = slots // 2
    last = planes - 1
    summed = parts[...].sum(0)
    lanes_at = lax.broadcasted_iota(jnp.int32, summed.shape, 1)
    c0, c1, c2, c3 = [
        jnp.where(lanes_at == at, summed, 0.0).sum(1, keepdims=True) for at in range(4)
    ]
    alpha = c0 / (c0 - c1)
    rest = 1.0 - alpha
    rz = rest * rest * c0 + 2.0 * alpha * rest * c1 + alpha * alpha * c2
    first = rest + rz / c0
    curve = first * first * (c0 - c1) + 2.0 * first * alpha * (c1 - c2) + alpha * alpha * (c2 - c3)
    step = rz / curve
    scale[0] = jnp.broadcast_to(alpha + step * first, (systems, lanes))
    scale[1] = jnp.broadcast_to(step * alpha, (systems, lanes))

    def slot_terms(s, fresh):
        ends = (s, slots + s)
        share = weight[pl.ds(s, 1)]
        on_z = [scale[0, pl.ds(e, 1)] for e in ends]
        on_n = [scale[1, pl.ds(e, 1)] for e in ends]

        def field(p):
            return [x[e, p] + on_z[i] * z[e, p] + on_n[i] * n[e, p] for i, e in enumerate(ends)]

        def outside():
            found = []
            for i, e in enumerate(ends):
                zm = ext_z[1, e]
                if s < half:
                    nm = ext_n[1, e]
                else:
                    w = lateral(zm, far[1, 2], far[1, 3]) + extra[s - half + i * half]
                    nm = far[1, 1] * (w + far[1, 0] * z[e, last])
                found.append(ext_x[1, e] + on_z[i] * zm + on_n[i] * nm)
            return found

        u, v = field(0)
        for p in range(planes):
            u_up, v_up = field(p + 1) if p < last else outside()
            face_x = kxf[p + 1] if p < last else far[1, 0]
            corr = face_x * (u_up - u) * (v_up - v)
            corr = corr + ky[p] * (next_y(u) - u) * (next_y(v) - v)
            corr = corr + kz[p] * (next_z(u) - u) * (next_z(v) - v)
            corr = corr + mass[p] * u * v
            total[p] = share * corr if fresh else total[p] + share * corr
            u, v = u_up, v_up

    for s in range(slots):
        slot_terms(s, s == 0)
    core = lax.rem(lax.axis_index("grp"), 2)
    deep = keep.shape[2]
    for at in range(keep.shape[0]):
        keep[at] = total[:, pl.ds(pl.multiple_of((2 * at + core) * deep, 8), deep)]
        give[at] = total[:, pl.ds(pl.multiple_of((2 * at + 1 - core) * deep, 8), deep)]


def merge_kernel(keep, got, own, to_1, to_2, to_3):
    mine = lax.div(lax.axis_index("grp"), 2)
    for at, out in enumerate((own, to_1, to_2, to_3)):
        block = jnp.bitwise_xor(mine, at)
        out[...] = keep[block] + got[block]


def total_kernel(own, one, two, three, out):
    out[...] = (own[...] + one[...]) + (two[...] + three[...])


def local(
    fwd_start, adj_start, adj_rhs, src_cell, group_count, region_label, cut_flag, region_sigma
):
    slots = fwd_start.shape[1]
    systems = 2 * slots
    planes, rows, lanes = region_label.shape
    groups = lax.axis_size("grp")
    tiles = lax.axis_size("tile")
    cells = planes * rows * lanes

    def held(*shape):
        return VMEM(shape, F32)

    def in_hbm(*arrays):
        return [pltpu.with_memory_space_constraint(a, pltpu.HBM) for a in arrays]

    def pinned(*arrays):
        return [pltpu.with_memory_space_constraint(a, pltpu.VMEM) for a in arrays]

    def params(**more):
        return pltpu.CompilerParams(vmem_limit_bytes=LIMIT, **more)

    half = slots // 2
    field = held(systems, planes, rows, lanes)
    plane_set = held(planes, rows, lanes)
    head = held(systems + 3, rows, lanes)
    message = held(systems + 2 * half, rows, lanes)
    HEAD, EDGES, INTERIOR, NEAR = 20, 20, 1, 10000

    def cost(scale):
        return pl.CostEstimate(flops=scale * cells, bytes_accessed=scale * cells, transcendentals=0)


    def opposite(value, parity):
        pairs = []
        for g in range(groups):
            by = 1 if g % 2 == parity else -1
            pairs += [(g * tiles + t, g * tiles + t + by) for t in range(tiles) if 0 <= t + by < tiles]
        return lax.ppermute(value, ("grp", "tile"), pairs)

    head_a, head_b, kxf, ky, kz, dd, inv, mass, weight = pl.pallas_call(
        head_kernel,
        out_shape=[
            head, head,
            held(planes + 1, rows, lanes),
            plane_set, plane_set, plane_set, plane_set, plane_set,
            held(8, lanes),
        ],
        in_specs=[IN_HBM, IN_SMEM] + [IN_HBM] * 4,
        out_specs=[IN_VMEM] * 9,
        scratch_shapes=[
            pltpu.SMEM(region_sigma.shape, F32),
            VMEM((planes, rows, lanes), jnp.int32),
            VMEM((planes, rows, lanes), jnp.int32),
            VMEM((planes, rows, lanes), F32),
            VMEM((planes, rows, lanes), F32),
            pltpu.SemaphoreType.DMA((7,)),
        ],
        compiler_params=params(),
        cost_estimate=cost(HEAD),
        name="head",
    )(
        *in_hbm(region_sigma), group_count,
        *in_hbm(fwd_start, adj_start, region_label, cut_flag),
    )
    near_a = opposite(head_a, 0)
    near_b = opposite(head_b, 1)

    msg_a, msg_b = pl.pallas_call(
        edges_kernel,
        out_shape=[message, message],
        in_specs=[IN_HBM] * 4 + [IN_VMEM] * 6,
        out_specs=[IN_VMEM] * 2,
        scratch_shapes=[
            pltpu.SMEM(src_cell.shape, jnp.int32),
            VMEM((systems, 4, rows, lanes), F32),
            VMEM((slots, 4, rows, lanes), F32),
            pltpu.SemaphoreType.DMA((7,)),
        ],
        compiler_params=params(),
        cost_estimate=cost(EDGES),
        name="edges",
    )(
        *in_hbm(src_cell, fwd_start, adj_start, adj_rhs),
        *pinned(head_a, head_b, kxf, ky, kz, inv),
    )
    got_a = opposite(msg_a, 0)
    got_b = opposite(msg_b, 1)

    x, z, n, moments, extra = pl.pallas_call(
        interior_kernel,
        out_shape=[field, field, field, held(systems, 4, 8, 128), held(2 * half, rows, lanes)],
        in_specs=[IN_HBM] * 4 + [IN_VMEM] * 5,
        out_specs=[IN_VMEM] * 5,
        scratch_shapes=[
            pltpu.SMEM(src_cell.shape, jnp.int32),
            VMEM((slots, planes, rows, lanes), F32),
            pltpu.SemaphoreType.DMA((4,)),
        ],
        compiler_params=params(),
        cost_estimate=cost(INTERIOR),
        name="interior",
    )(*in_hbm(src_cell, fwd_start, adj_start, adj_rhs), *pinned(kxf, ky, kz, dd, inv))

    pair_of = held(2, systems, rows, lanes)
    z, n, part, ext_x, far, moments = pl.pallas_call(
        near_kernel,
        out_shape=[field, field, pair_of, pair_of, held(2, 5, rows, lanes), held(systems, 4, 8, 128)],
        in_specs=[IN_VMEM] * 14,
        out_specs=[IN_VMEM] * 6,
        input_output_aliases={11: 0, 12: 1},
        scratch_shapes=[VMEM((2, rows, lanes), F32)],
        compiler_params=params(),
        cost_estimate=cost(NEAR),
        name="near",
    )(*pinned(near_a, near_b, head_a, head_b, msg_a, msg_b, kxf, ky, kz, dd, inv, z, n, moments))

    n, ext_z, ext_n, moments = pl.pallas_call(
        boundary_kernel,
        out_shape=[field, pair_of, pair_of, held(tiles, systems, 128)],
        in_specs=[IN_VMEM] * 13,
        out_specs=[IN_VMEM] * 4,
        input_output_aliases={11: 0},
        scratch_shapes=[VMEM((4, systems, 128), F32)],
        compiler_params=params(),
        name="boundary",
    )(*pinned(got_a, got_b, head_a, head_b, kxf, ky, kz, far, ext_x, part, z, n, moments))

    moments, extra = lax.optimization_barrier((moments, extra))
    late = lax.ppermute(extra, "tile", [(i + 1, i) for i in range(tiles - 1)])
    parts = lax.all_to_all(moments, "tile", 0, 0)

    blocks = held(groups // 2, planes, rows // groups, lanes)
    block = held(planes, rows // groups, lanes)
    keep, give = pl.pallas_call(
        correlate_kernel,
        out_shape=[blocks, blocks],
        in_specs=[IN_VMEM] * 14,
        out_specs=[IN_VMEM] * 2,
        scratch_shapes=[VMEM((2, systems, lanes), F32), VMEM((planes, rows, lanes), F32)],
        compiler_params=params(),
        name="correlate",
    )(*pinned(weight, parts, x, z, n, ext_x, ext_z, ext_n, far, late, kxf, ky, kz, mass))

    def swapped(value, by):
        return lax.ppermute(value, "grp", [(g, g ^ by) for g in range(groups)])

    got = swapped(give, 1)
    own, *sent = pl.pallas_call(
        merge_kernel,
        out_shape=[block] * 4,
        in_specs=[IN_VMEM] * 2,
        out_specs=[IN_VMEM] * 4,
        compiler_params=params(),
        name="merge",
    )(*pinned(keep, got))
    came = [swapped(value, 2 * (at + 1)) for at, value in enumerate(sent)]
    return pl.pallas_call(
        total_kernel,
        out_shape=jax.ShapeDtypeStruct((planes, rows // groups, lanes), F32),
        in_specs=[IN_VMEM] * 4,
        out_specs=IN_VMEM,
        compiler_params=params(),
        name="total",
    )(*pinned(own, *came))


def solution(mesh):
    in_specs = (
        P("grp", None, "tile", None, None),
        P("grp", None, "tile", None, None),
        P("grp", None, "tile", None, None),
        P("grp", None),
        P("grp"),
        P("tile", None, None),
        P("tile", None, None),
        P(),
    )
    out_specs = P("tile", "grp", None)
    return jax.shard_map(local, mesh=mesh, in_specs=in_specs, out_specs=out_specs, check_vma=False)
```

```python
import functools
import jax
import jax.numpy as jnp
from jax import lax
from jax.experimental import pallas as pl
from jax.experimental.pallas import tpu as pltpu
from jax.sharding import PartitionSpec as P

MASS = 0.05
SOURCE_AMP = 64.0
F32 = jnp.float32
VMEM = pltpu.VMEM
IN_SMEM = pl.BlockSpec(memory_space=pltpu.SMEM)
IN_VMEM = pl.BlockSpec(memory_space=pltpu.VMEM)
IN_HBM = pl.BlockSpec(memory_space=pltpu.HBM)
LIMIT = 24 * 1024 * 1024


def next_y(v):
    return pltpu.roll(v, v.shape[0] - 1, 0)


def prev_y(v):
    return pltpu.roll(v, 1, 0)


def next_z(v):
    return pltpu.roll(v, v.shape[1] - 1, 1)


def prev_z(v):
    return pltpu.roll(v, 1, 1)


def harmonic(left, right):
    return 2.0 * left * right / (left + right)


def harmonic_or_zero(left, right):
    return 2.0 * left * right / jnp.maximum(left + right, 1e-30)


def lateral_faces(sigma, factor, mean):
    rows = lax.broadcasted_iota(jnp.int32, sigma.shape, 0)
    lanes = lax.broadcasted_iota(jnp.int32, sigma.shape, 1)
    face_y = jnp.where(rows < sigma.shape[0] - 1, factor * mean(sigma, next_y(sigma)), 0.0)
    face_z = jnp.where(lanes < sigma.shape[1] - 1, factor * mean(sigma, next_z(sigma)), 0.0)
    return face_y, face_z


def lateral(v, face_y, face_z):
    return face_y * next_y(v) + prev_y(face_y * v) + face_z * next_z(v) + prev_z(face_z * v)


def upper_lateral(v, face_y, face_z):
    return face_y * next_y(v) + face_z * next_z(v)


def folded(v):
    rows, lanes = v.shape
    v = v.reshape(rows // 8, 8, lanes).sum(0)
    total = v[:, :128]
    for at in range(128, lanes, 128):
        total = total + v[:, at : at + 128]
    return total


def plane_source(src, slot, plane, shape):
    rows, lanes = shape
    planes = 8
    cell = src[0, slot] - (lax.axis_index("tile") * planes + plane) * (rows * lanes)
    at = lax.broadcasted_iota(jnp.int32, shape, 0) * lanes + lax.broadcasted_iota(jnp.int32, shape, 1)
    return jnp.where(at == cell, SOURCE_AMP, 0.0).astype(F32)


def conductivity(table, names):
    value = jnp.full(names.shape, table[0], F32)
    for region in range(1, table.shape[0]):
        value = jnp.where(names == region, table[region], value)
    return value


def cut_factor(flags):
    return 1.0 - 0.5 * flags.astype(F32)


def head_kernel(table_in, fwd, adj, label, cut, msg_a, msg_b, table, lab, flag, shared, sems):
    slots = fwd.shape[1]
    planes = label.shape[0]
    last = planes - 1
    systems = 2 * slots
    core = lax.rem(lax.axis_index("grp"), 2)
    front, back = pl.ds(0, 2), pl.ds(planes - 2, 2)
    copies = [
        pltpu.make_async_copy(table_in, table, sems.at[0]),
        pltpu.make_async_copy(label.at[front], lab.at[pl.ds(0, 2)], sems.at[1]),
        pltpu.make_async_copy(label.at[back], lab.at[pl.ds(2, 2)], sems.at[2]),
        pltpu.make_async_copy(cut.at[front], flag.at[pl.ds(0, 2)], sems.at[3]),
        pltpu.make_async_copy(cut.at[back], flag.at[pl.ds(2, 2)], sems.at[4]),
    ]
    edges = [(msg_a, core == 0), (msg_b, core == 1)]
    for at, (msg, up) in enumerate(edges):
        edge = jnp.where(up, last, 0)
        for half, source in enumerate((fwd, adj)):
            copies.append(
                pltpu.make_async_copy(
                    source.at[0, :, edge], msg.at[pl.ds(half * slots, slots)], sems.at[5 + 2 * at + half]
                )
            )
    for copy in copies:
        copy.start()
    for copy in copies[:5]:
        copy.wait()
    sigma = [conductivity(table, lab[at]) for at in range(4)]
    factor = [cut_factor(flag[at]) for at in range(4)]
    faces = [harmonic(sigma[at], sigma[at + 1]) * factor[at] for at in (0, 2)]
    for side, at in enumerate((0, 3)):
        face_y, face_z = lateral_faces(sigma[at], factor[at], harmonic)
        shared[side, 0] = sigma[at]
        shared[side, 1] = factor[at]
        diag = MASS * sigma[at] + faces[side] + face_y + prev_y(face_y) + face_z + prev_z(face_z)
        shared[side, 2] = diag
    for msg, up in edges:
        side = jnp.where(up, 1, 0)
        for at in range(3):
            msg[systems + at] = shared[side, at]
    for copy in copies[5:]:
        copy.wait()


def edges_kernel(
    table_in, src_in, count, fwd, adj, rhs_in, label, cut, head_a, head_b,
    msg_a, msg_b, x, rhs, kxf, ky, kz, dd, inv, sig, fac, weight,
    table, src, lab, flag, sems,
):
    slots = fwd.shape[1]
    systems = 2 * slots
    planes, rows, lanes = ky.shape
    last = planes - 1
    copies = [
        pltpu.make_async_copy(table_in, table, sems.at[0]),
        pltpu.make_async_copy(src_in, src, sems.at[1]),
        pltpu.make_async_copy(label, lab, sems.at[2]),
        pltpu.make_async_copy(cut, flag, sems.at[3]),
    ]
    spans = (pl.ds(0, 3), pl.ds(planes - 3, 3), pl.ds(3, planes - 6))
    for at, span in enumerate(spans):
        for half, source in enumerate((fwd, adj)):
            into = x.at[pl.ds(half * slots, slots), span]
            copies.append(pltpu.make_async_copy(source.at[0, :, span], into, sems.at[4 + 3 * at + half]))
        copies.append(pltpu.make_async_copy(rhs_in.at[0, :, span], rhs.at[:, span], sems.at[6 + 3 * at]))
    for copy in copies:
        copy.start()
    slot = lax.broadcasted_iota(jnp.int32, weight.shape, 0)
    weight[...] = jnp.where(slot < count[0], -1.0 / slots, 0.0).astype(F32)
    for copy in copies[:4]:
        copy.wait()

    @pl.loop(0, planes)
    def _(p):
        value = conductivity(table, lab[p])
        factor = cut_factor(flag[p])
        sig[p] = value
        fac[p] = factor
        face_y, face_z = lateral_faces(value, factor, harmonic)
        ky[p] = face_y
        kz[p] = face_z

    kxf[0] = jnp.zeros((rows, lanes), F32)
    kxf[planes] = jnp.zeros((rows, lanes), F32)

    @pl.loop(1, planes)
    def _(p):
        kxf[p] = harmonic(sig[p - 1], sig[p]) * fac[p - 1]

    @pl.loop(0, planes)
    def _(p):
        face_y, face_z = ky[p], kz[p]
        diag = MASS * sig[p] + kxf[p] + kxf[p + 1] + face_y + prev_y(face_y) + face_z + prev_z(face_z)
        dd[p] = diag
        inv[p] = 1.0 / diag

    for copy in copies[4:10]:
        copy.wait()
    core = lax.rem(lax.axis_index("grp"), 2)
    half = slots // 2
    for msg, up in ((msg_a, core == 0), (msg_b, core == 1)):
        edge, inner, third = jnp.where(up, last, 0), jnp.where(up, last - 1, 1), jnp.where(up, last - 2, 2)
        face, face_next = jnp.where(up, last, 1), jnp.where(up, last - 1, 2)
        lead = jnp.where(up, half, 0)

        def partial(s, right):
            msg[s] = right + lateral(x[s, edge], ky[edge], kz[edge]) + kxf[face] * x[s, inner]

        def onward(at, s, right):
            x1 = x[s, inner]
            total = right + lateral(x1, ky[inner], kz[inner])
            total = total + kxf[face] * x[s, edge] + kxf[face_next] * x[s, third]
            msg[systems + at] = kxf[face] * (inv[inner] * total - x1)

        @pl.loop(0, slots)
        def _(s):
            partial(s, plane_source(src, s, edge, (rows, lanes)))
            partial(slots + s, rhs[s, edge])

        @pl.loop(0, half)
        def _(s):
            slot = lead + s
            onward(s, slot, plane_source(src, slot, inner, (rows, lanes)))
            onward(half + s, slots + slot, rhs[slot, inner])

    for copy in copies[10:]:
        copy.wait()


def interior_kernel(src_in, x, rs, kxf, ky, kz, dd, inv, z, n, moments, extra, src, sem):
    systems, planes, rows, lanes = x.shape
    slots = systems // 2
    last = planes - 1
    fetch = pltpu.make_async_copy(src_in, src, sem)
    fetch.start()
    fetch.wait()

    def one(s, right):
        for p in range(1, last):
            total = right(p) + lateral(x[s, p], ky[p], kz[p])
            total = total + kxf[p] * x[s, p - 1] + kxf[p + 1] * x[s, p + 1]
            z[s, p] = inv[p] * total - x[s, p]
        c0 = jnp.zeros((8, 128), F32)
        c1, c2, c3 = c0, c0, c0
        for p in range(1, last):
            v = z[s, p]
            c0 = c0 + folded(dd[p] * v * v)
            w = lateral(v, ky[p], kz[p])
            if p > 1:
                w = w + kxf[p] * z[s, p - 1]
            if p < last - 1:
                w = w + kxf[p + 1] * z[s, p + 1]
            if p == 1 or p == last - 1:
                n[s, p] = w
                continue
            m = inv[p] * w
            n[s, p] = m
            c1 = c1 + folded(v * w)
            c2 = c2 + folded(m * w)
            near = upper_lateral(m, ky[p], kz[p])
            if p > 2:
                near = near + kxf[p] * n[s, p - 1]
            c3 = c3 + folded(m * near)
        for at, c in enumerate((c0, c1, c2, c3)):
            moments[s, at] = c

    @pl.loop(0, slots)
    def _(s):
        one(s, lambda p: plane_source(src, s, p, (rows, lanes)))

    @pl.loop(0, slots)
    def _(s):
        one(slots + s, lambda p: rs[s, p])

    half = slots // 2
    for at in range(half):
        extra[at] = kxf[1] * z[half + at, 1]
        extra[half + at] = kxf[1] * z[slots + half + at, 1]


def both_sides(planes, slots, pairs):
    last, half = planes - 1, slots // 2
    core = lax.rem(lax.axis_index("grp"), 2)
    found = []
    for at, pair in enumerate(pairs):
        low = core == at
        found.append(
            (
                at, pair, low, jnp.where(low, 0, 1),
                jnp.where(low, 0, last), jnp.where(low, 1, last - 1), jnp.where(low, 2, last - 2),
                jnp.where(low, 1, last), jnp.where(low, 2, last - 1), jnp.where(low, half, 0),
            )
        )
    return found


def near_kernel(
    got_a, got_b, head_a, head_b, msg_a, msg_b, kxf, ky, kz, dd, inv, z_in, n_in, moments_in,
    z, n, part, ext_x, far, moments,
    coef,
):
    systems, planes, rows, lanes = z.shape
    sides = both_sides(planes, systems // 2, ((got_a, head_b, msg_b), (got_b, head_a, msg_a)))
    for at, (got, head, _), low, side, edge, _, _, _, _, _ in sides:
        cross = harmonic(got[systems], head[systems])
        cross = cross * jnp.where(low, got[systems + 1], head[systems + 1])
        here = dd[edge] + cross
        there = got[systems + 2] + cross
        real = there > 0.0
        coef[at] = here
        far[side, 0] = cross
        far[side, 1] = jnp.where(real, 1.0 / jnp.where(real, there, 1.0), 0.0)
        face_y, face_z = lateral_faces(got[systems], got[systems + 1], harmonic_or_zero)
        far[side, 2] = face_y
        far[side, 3] = face_z
        far[side, 4] = 1.0 / here

    @pl.loop(0, systems)
    def _(s):
        c0, c1, c2, c3 = [moments_in[s, at] for at in range(4)]
        for at, (got, head, msg), _, side, edge, inner, third, face, face_next, _ in sides:
            xm = got[s]
            z0 = far[side, 4] * (msg[s] + far[side, 0] * xm) - head[s]
            z1 = z_in[s, inner]
            w0 = lateral(z0, ky[edge], kz[edge]) + kxf[face] * z1
            w1 = n_in[s, inner] + kxf[face] * z0
            n1 = inv[inner] * w1
            z[s, edge] = z0
            n[s, inner] = n1
            part[side, s] = w0
            ext_x[side, s] = xm
            c0 = c0 + folded(coef[at] * z0 * z0)
            c1 = c1 + folded(z0 * w0 + z1 * w1)
            c2 = c2 + folded(n1 * w1)
            near1 = upper_lateral(n1, ky[inner], kz[inner]) + kxf[face_next] * n_in[s, third]
            c3 = c3 + folded(n1 * near1)
        for at, c in enumerate((c0, c1, c2, c3)):
            moments[s, at] = c


def boundary_kernel(
    got_a, got_b, head_a, head_b, kxf, ky, kz, far, ext_x, part, z, n_in, moments,
    n, ext_z, ext_n, out,
    sums,
):
    systems, planes, rows, lanes = n.shape
    slots = systems // 2
    half = slots // 2
    sides = both_sides(planes, slots, ((got_a, head_b), (got_b, head_a)))

    @pl.loop(0, systems)
    def _(s):
        c0, c1, c2, c3 = [moments[s, at] for at in range(4)]
        for _, (got, head), _, side, edge, inner, _, face, _, _ in sides:
            cross = far[side, 0]
            z0 = z[s, edge]
            zm = far[side, 1] * (got[s] + cross * head[s]) - ext_x[side, s]
            over = cross * zm
            w0 = part[side, s] + over
            n0 = far[side, 4] * w0
            n[s, edge] = n0
            ext_z[side, s] = zm
            c1 = c1 + folded(z0 * over)
            c2 = c2 + folded(n0 * w0)
            near0 = upper_lateral(n0, ky[edge], kz[edge]) + kxf[face] * n_in[s, inner]
            c3 = c3 + folded(n0 * near0)
        for at, c in enumerate((c0, c1, c2, c3 + c3)):
            sums[at, pl.ds(s, 1)] = c.sum(0, keepdims=True)

    @pl.loop(0, half)
    def _(at):
        for _, (got, _), _, side, edge, _, _, _, _, lead in sides:
            for place, s in ((at, lead + at), (half + at, slots + lead + at)):
                cross = far[side, 0]
                w = lateral(ext_z[side, s], far[side, 2], far[side, 3])
                w = w + got[systems + place] + cross * z[s, edge]
                nm = far[side, 1] * w
                ext_n[side, s] = nm
                pair = folded(cross * nm * n[s, edge])
                sums[3, pl.ds(s, 1)] = sums[3, pl.ds(s, 1)] + 2.0 * pair.sum(0, keepdims=True)

    lanes_at = lax.broadcasted_iota(jnp.int32, (systems, 128), 1)
    packed = jnp.zeros((systems, 128), F32)
    for at in range(4):
        packed = packed + jnp.where(lanes_at == at, sums[at].sum(1, keepdims=True), 0.0)
    out[...] = jnp.broadcast_to(packed[None], out.shape)


def steps_kernel(parts, scale):
    summed = parts[...].sum(0)
    lanes_at = lax.broadcasted_iota(jnp.int32, summed.shape, 1)
    c0, c1, c2, c3 = [
        jnp.where(lanes_at == at, summed, 0.0).sum(1, keepdims=True) for at in range(4)
    ]
    alpha = c0 / (c0 - c1)
    rest = 1.0 - alpha
    rz = rest * rest * c0 + 2.0 * alpha * rest * c1 + alpha * alpha * c2
    first = rest + rz / c0
    curve = first * first * (c0 - c1) + 2.0 * first * alpha * (c1 - c2) + alpha * alpha * (c2 - c3)
    step = rz / curve
    scale[0] = jnp.broadcast_to(alpha + step * first, scale.shape[1:])
    scale[1] = jnp.broadcast_to(step * alpha, scale.shape[1:])


def correlate_kernel(
    weight, scale, x, z, n, ext_x, ext_z, ext_n, far, extra, kxf, ky, kz, sig, keep, give, total
):
    systems, planes, rows, lanes = z.shape
    slots = systems // 2
    half = slots // 2
    last = planes - 1

    def slot_terms(s, fresh):
        ends = (s, slots + s)
        share = weight[pl.ds(s, 1)]
        on_z = [scale[0, pl.ds(e, 1)] for e in ends]
        on_n = [scale[1, pl.ds(e, 1)] for e in ends]

        def field(p):
            return [x[e, p] + on_z[i] * z[e, p] + on_n[i] * n[e, p] for i, e in enumerate(ends)]

        def outside():
            found = []
            for i, e in enumerate(ends):
                zm = ext_z[1, e]
                if s < half:
                    nm = ext_n[1, e]
                else:
                    w = lateral(zm, far[1, 2], far[1, 3]) + extra[s - half + i * half]
                    nm = far[1, 1] * (w + far[1, 0] * z[e, last])
                found.append(ext_x[1, e] + on_z[i] * zm + on_n[i] * nm)
            return found

        u, v = field(0)
        for p in range(planes):
            u_up, v_up = field(p + 1) if p < last else outside()
            face_x = kxf[p + 1] if p < last else far[1, 0]
            corr = face_x * (u_up - u) * (v_up - v)
            corr = corr + ky[p] * (next_y(u) - u) * (next_y(v) - v)
            corr = corr + kz[p] * (next_z(u) - u) * (next_z(v) - v)
            corr = corr + (MASS * sig[p]) * u * v
            total[p] = share * corr if fresh else total[p] + share * corr
            u, v = u_up, v_up

    for s in range(slots):
        slot_terms(s, s == 0)
    core = lax.rem(lax.axis_index("grp"), 2)
    deep = keep.shape[2]
    for at in range(keep.shape[0]):
        keep[at] = total[:, pl.ds(pl.multiple_of((2 * at + core) * deep, 8), deep)]
        give[at] = total[:, pl.ds(pl.multiple_of((2 * at + 1 - core) * deep, 8), deep)]


def merge_kernel(keep, got, own, to_1, to_2, to_3):
    mine = lax.div(lax.axis_index("grp"), 2)
    for at, out in enumerate((own, to_1, to_2, to_3)):
        block = jnp.bitwise_xor(mine, at)
        out[...] = keep[block] + got[block]


def total_kernel(own, one, two, three, out):
    out[...] = (own[...] + one[...]) + (two[...] + three[...])


def local(
    fwd_start, adj_start, adj_rhs, src_cell, group_count, region_label, cut_flag, region_sigma
):
    slots = fwd_start.shape[1]
    systems = 2 * slots
    planes, rows, lanes = region_label.shape
    groups = lax.axis_size("grp")
    tiles = lax.axis_size("tile")
    cells = planes * rows * lanes

    def held(*shape):
        return VMEM(shape, F32)

    def in_hbm(*arrays):
        return [pltpu.with_memory_space_constraint(a, pltpu.HBM) for a in arrays]

    def pinned(*arrays):
        return [pltpu.with_memory_space_constraint(a, pltpu.VMEM) for a in arrays]

    def params(**more):
        return pltpu.CompilerParams(vmem_limit_bytes=LIMIT, **more)

    half = slots // 2
    field = held(systems, planes, rows, lanes)
    plane_set = held(planes, rows, lanes)
    head = held(systems + 3, rows, lanes)
    message = held(systems + 2 * half, rows, lanes)
    HEAD, EDGES, INTERIOR, NEAR, STEPS = 20, 20, 1, 10000, 1

    def cost(scale):
        return pl.CostEstimate(flops=scale * cells, bytes_accessed=scale * cells, transcendentals=0)


    def opposite(value, parity):
        pairs = []
        for g in range(groups):
            by = 1 if g % 2 == parity else -1
            pairs += [(g * tiles + t, g * tiles + t + by) for t in range(tiles) if 0 <= t + by < tiles]
        return lax.ppermute(value, ("grp", "tile"), pairs)

    head_a, head_b = pl.pallas_call(
        head_kernel,
        out_shape=[head, head],
        in_specs=[IN_HBM] * 5,
        out_specs=[IN_VMEM] * 2,
        scratch_shapes=[
            pltpu.SMEM(region_sigma.shape, F32),
            VMEM((4, rows, lanes), jnp.int32),
            VMEM((4, rows, lanes), jnp.int32),
            VMEM((2, 3, rows, lanes), F32),
            pltpu.SemaphoreType.DMA((9,)),
        ],
        compiler_params=params(),
        cost_estimate=cost(HEAD),
        name="head",
    )(*in_hbm(region_sigma, fwd_start, adj_start, region_label, cut_flag))
    near_a = opposite(head_a, 0)
    near_b = opposite(head_b, 1)

    msg_a, msg_b, x, rhs, kxf, ky, kz, dd, inv, sig, fac, weight = pl.pallas_call(
        edges_kernel,
        out_shape=[
            message, message, field, held(slots, planes, rows, lanes),
            held(planes + 1, rows, lanes),
            plane_set, plane_set, plane_set, plane_set, plane_set, plane_set,
            held(8, lanes),
        ],
        in_specs=[IN_HBM] * 2 + [IN_SMEM] + [IN_HBM] * 5 + [IN_VMEM] * 2,
        out_specs=[IN_VMEM] * 12,
        scratch_shapes=[
            pltpu.SMEM(region_sigma.shape, F32),
            pltpu.SMEM(src_cell.shape, jnp.int32),
            VMEM((planes, rows, lanes), jnp.int32),
            VMEM((planes, rows, lanes), jnp.int32),
            pltpu.SemaphoreType.DMA((13,)),
        ],
        compiler_params=params(),
        cost_estimate=cost(EDGES),
        name="edges",
    )(
        *in_hbm(region_sigma, src_cell), group_count,
        *in_hbm(fwd_start, adj_start, adj_rhs, region_label, cut_flag),
        *pinned(head_a, head_b),
    )
    got_a = opposite(msg_a, 0)
    got_b = opposite(msg_b, 1)

    z, n, moments, extra = pl.pallas_call(
        interior_kernel,
        out_shape=[field, field, held(systems, 4, 8, 128), held(2 * half, rows, lanes)],
        in_specs=[IN_HBM] + [IN_VMEM] * 7,
        out_specs=[IN_VMEM] * 4,
        scratch_shapes=[pltpu.SMEM(src_cell.shape, jnp.int32), pltpu.SemaphoreType.DMA],
        compiler_params=params(),
        cost_estimate=cost(INTERIOR),
        name="interior",
    )(*in_hbm(src_cell), *pinned(x, rhs, kxf, ky, kz, dd, inv))

    pair_of = held(2, systems, rows, lanes)
    z, n, part, ext_x, far, moments = pl.pallas_call(
        near_kernel,
        out_shape=[field, field, pair_of, pair_of, held(2, 5, rows, lanes), held(systems, 4, 8, 128)],
        in_specs=[IN_VMEM] * 14,
        out_specs=[IN_VMEM] * 6,
        input_output_aliases={11: 0, 12: 1},
        scratch_shapes=[VMEM((2, rows, lanes), F32)],
        compiler_params=params(),
        cost_estimate=cost(NEAR),
        name="near",
    )(*pinned(near_a, near_b, head_a, head_b, msg_a, msg_b, kxf, ky, kz, dd, inv, z, n, moments))

    moments, extra = lax.optimization_barrier((moments, extra))
    late = lax.ppermute(extra, "tile", [(i + 1, i) for i in range(tiles - 1)])

    n, ext_z, ext_n, moments = pl.pallas_call(
        boundary_kernel,
        out_shape=[field, pair_of, pair_of, held(tiles, systems, 128)],
        in_specs=[IN_VMEM] * 13,
        out_specs=[IN_VMEM] * 4,
        input_output_aliases={11: 0},
        scratch_shapes=[VMEM((4, systems, 128), F32)],
        compiler_params=params(),
        name="boundary",
    )(*pinned(got_a, got_b, head_a, head_b, kxf, ky, kz, far, ext_x, part, z, n, moments))

    parts = lax.all_to_all(moments, "tile", 0, 0)

    blocks = held(groups // 2, planes, rows // groups, lanes)
    block = held(planes, rows // groups, lanes)
    scale = pl.pallas_call(
        steps_kernel,
        out_shape=held(2, systems, lanes),
        in_specs=[IN_VMEM],
        out_specs=IN_VMEM,
        compiler_params=params(),
        cost_estimate=cost(STEPS),
        name="steps",
    )(*pinned(parts))
    keep, give = pl.pallas_call(
        correlate_kernel,
        out_shape=[blocks, blocks],
        in_specs=[IN_VMEM] * 14,
        out_specs=[IN_VMEM] * 2,
        scratch_shapes=[VMEM((planes, rows, lanes), F32)],
        compiler_params=params(),
        name="correlate",
    )(*pinned(weight, scale, x, z, n, ext_x, ext_z, ext_n, far, late, kxf, ky, kz, sig))

    def swapped(value, by):
        return lax.ppermute(value, "grp", [(g, g ^ by) for g in range(groups)])

    got = swapped(give, 1)
    own, *sent = pl.pallas_call(
        merge_kernel,
        out_shape=[block] * 4,
        in_specs=[IN_VMEM] * 2,
        out_specs=[IN_VMEM] * 4,
        compiler_params=params(),
        name="merge",
    )(*pinned(keep, got))
    came = [swapped(value, 2 * (at + 1)) for at, value in enumerate(sent)]
    return pl.pallas_call(
        total_kernel,
        out_shape=jax.ShapeDtypeStruct((planes, rows // groups, lanes), F32),
        in_specs=[IN_VMEM] * 4,
        out_specs=IN_VMEM,
        compiler_params=params(),
        name="total",
    )(*pinned(own, *came))


def solution(mesh):
    in_specs = (
        P("grp", None, "tile", None, None),
        P("grp", None, "tile", None, None),
        P("grp", None, "tile", None, None),
        P("grp", None),
        P("grp"),
        P("tile", None, None),
        P("tile", None, None),
        P(),
    )
    out_specs = P("tile", "grp", None)
    return jax.shard_map(local, mesh=mesh, in_specs=in_specs, out_specs=out_specs, check_vma=False)
```

```python
import functools
import jax
import jax.numpy as jnp
from jax import lax
from jax.experimental import pallas as pl
from jax.experimental.pallas import tpu as pltpu
from jax.sharding import PartitionSpec as P

MASS = 0.05
SOURCE_AMP = 64.0
F32 = jnp.float32
VMEM = pltpu.VMEM
IN_SMEM = pl.BlockSpec(memory_space=pltpu.SMEM)
IN_VMEM = pl.BlockSpec(memory_space=pltpu.VMEM)
IN_HBM = pl.BlockSpec(memory_space=pltpu.HBM)
LIMIT = 24 * 1024 * 1024


def next_y(v):
    return pltpu.roll(v, v.shape[0] - 1, 0)


def prev_y(v):
    return pltpu.roll(v, 1, 0)


def next_z(v):
    return pltpu.roll(v, v.shape[1] - 1, 1)


def prev_z(v):
    return pltpu.roll(v, 1, 1)


def harmonic(left, right):
    return 2.0 * left * right / (left + right)


def harmonic_or_zero(left, right):
    return 2.0 * left * right / jnp.maximum(left + right, 1e-30)


def lateral_faces(sigma, factor, mean):
    rows = lax.broadcasted_iota(jnp.int32, sigma.shape, 0)
    lanes = lax.broadcasted_iota(jnp.int32, sigma.shape, 1)
    face_y = jnp.where(rows < sigma.shape[0] - 1, factor * mean(sigma, next_y(sigma)), 0.0)
    face_z = jnp.where(lanes < sigma.shape[1] - 1, factor * mean(sigma, next_z(sigma)), 0.0)
    return face_y, face_z


def lateral(v, face_y, face_z, back_z):
    flow_y = face_y * (next_y(v) - v)
    along_z = face_z * (next_z(v) - v) + back_z * (prev_z(v) - v)
    return (flow_y - prev_y(flow_y)) + along_z


def upper_lateral(v, face_y, face_z):
    return face_y * next_y(v) + face_z * next_z(v)


def folded(v):
    rows, lanes = v.shape
    v = v.reshape(rows // 8, 8, lanes).sum(0)
    total = v[:, :128]
    for at in range(128, lanes, 128):
        total = total + v[:, at : at + 128]
    return total


def plane_source(src, slot, plane, shape):
    rows, lanes = shape
    planes = 8
    cell = src[0, slot] - (lax.axis_index("tile") * planes + plane) * (rows * lanes)
    at = lax.broadcasted_iota(jnp.int32, shape, 0) * lanes + lax.broadcasted_iota(jnp.int32, shape, 1)
    return jnp.where(at == cell, SOURCE_AMP, 0.0).astype(F32)


def conductivity(table, names):
    value = jnp.full(names.shape, table[0], F32)
    for region in range(1, table.shape[0]):
        value = jnp.where(names == region, table[region], value)
    return value


def cut_factor(flags):
    return 1.0 - 0.5 * flags.astype(F32)


def head_kernel(table_in, fwd, adj, label, cut, msg_a, msg_b, table, lab, flag, shared, sems):
    slots = fwd.shape[1]
    planes = label.shape[0]
    last = planes - 1
    systems = 2 * slots
    core = lax.rem(lax.axis_index("grp"), 2)
    front, back = pl.ds(0, 2), pl.ds(planes - 2, 2)
    copies = [
        pltpu.make_async_copy(table_in, table, sems.at[0]),
        pltpu.make_async_copy(label.at[front], lab.at[pl.ds(0, 2)], sems.at[1]),
        pltpu.make_async_copy(label.at[back], lab.at[pl.ds(2, 2)], sems.at[2]),
        pltpu.make_async_copy(cut.at[front], flag.at[pl.ds(0, 2)], sems.at[3]),
        pltpu.make_async_copy(cut.at[back], flag.at[pl.ds(2, 2)], sems.at[4]),
    ]
    edges = [(msg_a, core == 0), (msg_b, core == 1)]
    for at, (msg, up) in enumerate(edges):
        edge = jnp.where(up, last, 0)
        for half, source in enumerate((fwd, adj)):
            copies.append(
                pltpu.make_async_copy(
                    source.at[0, :, edge], msg.at[pl.ds(half * slots, slots)], sems.at[5 + 2 * at + half]
                )
            )
    for copy in copies:
        copy.start()
    for copy in copies[:5]:
        copy.wait()
    sigma = [conductivity(table, lab[at]) for at in range(4)]
    factor = [cut_factor(flag[at]) for at in range(4)]
    faces = [harmonic(sigma[at], sigma[at + 1]) * factor[at] for at in (0, 2)]
    for side, at in enumerate((0, 3)):
        shared[side, 0] = sigma[at]
        shared[side, 1] = factor[at]
        shared[side, 2] = faces[side]
    for msg, up in edges:
        side = jnp.where(up, 1, 0)
        for at in range(3):
            msg[systems + at] = shared[side, at]
    for copy in copies[5:]:
        copy.wait()


def edges_kernel(
    table_in, src_in, count, fwd, adj, rhs_in, label, cut, head_a, head_b,
    msg_a, msg_b, x, rhs, kxf, ky, kz, dd, inv, mass, kzb, weight,
    table, src, lab, flag, sig, fac, sems,
):
    slots = fwd.shape[1]
    systems = 2 * slots
    planes, rows, lanes = ky.shape
    last = planes - 1
    copies = [
        pltpu.make_async_copy(table_in, table, sems.at[0]),
        pltpu.make_async_copy(src_in, src, sems.at[1]),
        pltpu.make_async_copy(label, lab, sems.at[2]),
        pltpu.make_async_copy(cut, flag, sems.at[3]),
    ]
    spans = (pl.ds(0, 3), pl.ds(planes - 3, 3), pl.ds(3, planes - 6))
    for at, span in enumerate(spans):
        for half, source in enumerate((fwd, adj)):
            into = x.at[pl.ds(half * slots, slots), span]
            copies.append(pltpu.make_async_copy(source.at[0, :, span], into, sems.at[4 + 3 * at + half]))
        copies.append(pltpu.make_async_copy(rhs_in.at[0, :, span], rhs.at[:, span], sems.at[6 + 3 * at]))
    for copy in copies:
        copy.start()
    slot = lax.broadcasted_iota(jnp.int32, weight.shape, 0)
    weight[...] = jnp.where(slot < count[0], -1.0 / slots, 0.0).astype(F32)
    for copy in copies[:4]:
        copy.wait()

    @pl.loop(0, planes)
    def _(p):
        value = conductivity(table, lab[p])
        factor = cut_factor(flag[p])
        sig[p] = value
        fac[p] = factor
        mass[p] = MASS * value
        face_y, face_z = lateral_faces(value, factor, harmonic)
        ky[p] = face_y
        kz[p] = face_z
        kzb[p] = prev_z(face_z)

    kxf[0] = jnp.zeros((rows, lanes), F32)
    kxf[planes] = jnp.zeros((rows, lanes), F32)

    @pl.loop(1, planes)
    def _(p):
        kxf[p] = harmonic(sig[p - 1], sig[p]) * fac[p - 1]

    @pl.loop(0, planes)
    def _(p):
        face_y = ky[p]
        diag = mass[p] + kxf[p] + kxf[p + 1] + face_y + prev_y(face_y) + kz[p] + kzb[p]
        dd[p] = diag
        inv[p] = 1.0 / diag

    for copy in copies[4:10]:
        copy.wait()
    core = lax.rem(lax.axis_index("grp"), 2)
    half = slots // 2
    for msg, up in ((msg_a, core == 0), (msg_b, core == 1)):
        edge, inner, third = jnp.where(up, last, 0), jnp.where(up, last - 1, 1), jnp.where(up, last - 2, 2)
        face, face_next = jnp.where(up, last, 1), jnp.where(up, last - 1, 2)
        lead = jnp.where(up, half, 0)

        def partial(s, right):
            x0 = x[s, edge]
            total = right - mass[edge] * x0 + lateral(x0, ky[edge], kz[edge], kzb[edge])
            msg[s] = total + kxf[face] * (x[s, inner] - x0)

        def onward(at, s, right):
            x1 = x[s, inner]
            total = right - mass[inner] * x1 + lateral(x1, ky[inner], kz[inner], kzb[inner])
            total = total + kxf[face] * (x[s, edge] - x1) + kxf[face_next] * (x[s, third] - x1)
            msg[systems + at] = inv[inner] * total

        @pl.loop(0, slots)
        def _(s):
            partial(s, plane_source(src, s, edge, (rows, lanes)))
            partial(slots + s, rhs[s, edge])

        @pl.loop(0, half)
        def _(s):
            slot = lead + s
            onward(s, slot, plane_source(src, slot, inner, (rows, lanes)))
            onward(half + s, slots + slot, rhs[slot, inner])

    for copy in copies[10:]:
        copy.wait()


def interior_kernel(src_in, x, rs, kxf, ky, kz, mass, inv, kzb, z, n, moments, extra, src, sem):
    systems, planes, rows, lanes = x.shape
    slots = systems // 2
    last = planes - 1
    fetch = pltpu.make_async_copy(src_in, src, sem)
    fetch.start()
    fetch.wait()

    def one(s, right):
        zero = jnp.zeros((8, 128), F32)
        c0, c1, c2, c3 = zero, zero, zero, zero
        for p in range(1, last):
            v = x[s, p]
            total = right(p) - mass[p] * v + lateral(v, ky[p], kz[p], kzb[p])
            total = total + kxf[p + 1] * (x[s, p + 1] - v) + kxf[p] * (x[s, p - 1] - v)
            fresh = inv[p] * total
            z[s, p] = fresh
            c0 = c0 + folded(fresh * total)
        for p in range(1, last):
            v = z[s, p]
            w = mass[p] * v - lateral(v, ky[p], kz[p], kzb[p])
            if p < last - 1:
                w = w - kxf[p + 1] * (z[s, p + 1] - v)
            if p > 1:
                w = w - kxf[p] * (z[s, p - 1] - v)
            if p == 1 or p == last - 1:
                n[s, p] = w
                continue
            m = inv[p] * w
            n[s, p] = m
            c1 = c1 + folded(v * w)
            c2 = c2 + folded(m * w)
            near = upper_lateral(m, ky[p], kz[p])
            if p > 2:
                near = near + kxf[p] * n[s, p - 1]
            c3 = c3 + folded(m * near)
        for at, c in enumerate((c0, c1, c2, c3)):
            moments[s, at] = c

    @pl.loop(0, slots)
    def _(s):
        one(s, lambda p: plane_source(src, s, p, (rows, lanes)))

    @pl.loop(0, slots)
    def _(s):
        one(slots + s, lambda p: rs[s, p])

    half = slots // 2
    for at in range(half):
        extra[at] = z[half + at, 1]
        extra[half + at] = z[slots + half + at, 1]


def both_sides(planes, slots, pairs):
    last, half = planes - 1, slots // 2
    core = lax.rem(lax.axis_index("grp"), 2)
    found = []
    for at, pair in enumerate(pairs):
        low = core == at
        found.append(
            (
                at, pair, low, jnp.where(low, 0, 1),
                jnp.where(low, 0, last), jnp.where(low, 1, last - 1), jnp.where(low, 2, last - 2),
                jnp.where(low, 1, last), jnp.where(low, 2, last - 1), jnp.where(low, half, 0),
            )
        )
    return found


def near_kernel(
    got_a, got_b, head_a, head_b, msg_a, msg_b, kxf, ky, kz, dd, inv, z_in, n_in, moments_in, mass, kzb,
    z, n, part, ext_x, far, moments,
):
    systems, planes, rows, lanes = z.shape
    sides = both_sides(planes, systems // 2, ((got_a, head_b, msg_b), (got_b, head_a, msg_a)))
    for at, (got, head, _), low, side, edge, _, _, _, _, _ in sides:
        sigma, factor, beyond = got[systems], got[systems + 1], got[systems + 2]
        cross = harmonic(sigma, head[systems]) * jnp.where(low, factor, head[systems + 1])
        face_y, face_z = lateral_faces(sigma, factor, harmonic_or_zero)
        there = MASS * sigma + beyond + cross
        back_z = prev_z(face_z)
        there = there + face_y + prev_y(face_y) + face_z + back_z
        real = there > 0.0
        far[side, 0] = cross
        far[side, 1] = jnp.where(real, 1.0 / jnp.where(real, there, 1.0), 0.0)
        far[side, 2] = face_y
        far[side, 3] = face_z
        far[side, 4] = 1.0 / (dd[edge] + cross)
        far[side, 5] = MASS * sigma
        far[side, 6] = beyond
        far[side, 7] = back_z

    @pl.loop(0, systems)
    def _(s):
        c0, c1, c2, c3 = [moments_in[s, at] for at in range(4)]
        for at, (got, head, msg), _, side, edge, inner, third, face, face_next, _ in sides:
            xm = got[s]
            total = msg[s] + far[side, 0] * (xm - head[s])
            z0 = far[side, 4] * total
            z1 = z_in[s, inner]
            flow = kxf[face] * (z1 - z0)
            w0 = mass[edge] * z0 - lateral(z0, ky[edge], kz[edge], kzb[edge]) - flow
            w1 = n_in[s, inner] + flow
            n1 = inv[inner] * w1
            z[s, edge] = z0
            n[s, inner] = n1
            part[side, s] = w0
            ext_x[side, s] = xm
            c0 = c0 + folded(total * z0)
            c1 = c1 + folded(z0 * w0 + z1 * w1)
            c2 = c2 + folded(n1 * w1)
            near = upper_lateral(n1, ky[inner], kz[inner]) + kxf[face_next] * n_in[s, third]
            c3 = c3 + folded(n1 * near)
        for at, c in enumerate((c0, c1, c2, c3)):
            moments[s, at] = c


def outer_slope(v, beyond, edge, far, side):
    w = far[side, 5] * v - lateral(v, far[side, 2], far[side, 3], far[side, 7])
    w = w - far[side, 6] * (beyond - v) - far[side, 0] * (edge - v)
    return far[side, 1] * w


def boundary_kernel(
    got_a, got_b, head_a, head_b, kxf, ky, kz, far, ext_x, part, z, n_in, moments,
    n, ext_z, ext_n, out,
    sums,
):
    systems, planes, rows, lanes = n.shape
    slots = systems // 2
    half = slots // 2
    sides = both_sides(planes, slots, ((got_a, head_b), (got_b, head_a)))

    @pl.loop(0, systems)
    def _(s):
        c0, c1, c2, c3 = [moments[s, at] for at in range(4)]
        for _, (got, head), _, side, edge, inner, _, face, _, _ in sides:
            cross = far[side, 0]
            z0 = z[s, edge]
            zm = far[side, 1] * (got[s] + cross * (head[s] - ext_x[side, s]))
            over = cross * (zm - z0)
            w0 = part[side, s] - over
            n0 = far[side, 4] * w0
            n[s, edge] = n0
            ext_z[side, s] = zm
            c1 = c1 - folded(z0 * over)
            c2 = c2 + folded(n0 * w0)
            near = upper_lateral(n0, ky[edge], kz[edge]) + kxf[face] * n_in[s, inner]
            c3 = c3 + folded(n0 * near)
        for at, c in enumerate((c0, c1, c2, c3 + c3)):
            sums[at, pl.ds(s, 1)] = c.sum(0, keepdims=True)

    @pl.loop(0, half)
    def _(at):
        for _, (got, _), _, side, edge, _, _, _, _, lead in sides:
            for place, s in ((at, lead + at), (half + at, slots + lead + at)):
                nm = outer_slope(ext_z[side, s], got[systems + place], z[s, edge], far, side)
                ext_n[side, s] = nm
                pair = folded(far[side, 0] * nm * n[s, edge])
                sums[3, pl.ds(s, 1)] = sums[3, pl.ds(s, 1)] + 2.0 * pair.sum(0, keepdims=True)

    lanes_at = lax.broadcasted_iota(jnp.int32, (systems, 128), 1)
    packed = jnp.zeros((systems, 128), F32)
    for at in range(4):
        packed = packed + jnp.where(lanes_at == at, sums[at].sum(1, keepdims=True), 0.0)
    out[...] = jnp.broadcast_to(packed[None], out.shape)


def steps_kernel(parts, scale):
    summed = parts[...].sum(0)
    lanes_at = lax.broadcasted_iota(jnp.int32, summed.shape, 1)
    m0, m1, m2, c3 = [
        jnp.where(lanes_at == at, summed, 0.0).sum(1, keepdims=True) for at in range(4)
    ]
    unit = 1.0 / m1
    m0, m1, m2, c3 = m0 * unit, m1 * unit, m2 * unit, c3 * unit
    alpha = m0 / m1
    top = m0 * (m2 - m1) + m1 * (m0 - m1)
    low = -m1 * c3 - m2 * (m2 - m1)
    real = jnp.logical_and(top > 0.0, low > 0.0)
    step = jnp.where(real, top * m1 / jnp.where(real, m0 * low, 1.0), 0.0)
    grown = 1.0 + top / (m1 * m1)
    scale[0] = jnp.broadcast_to(alpha + step * grown, scale.shape[1:])
    scale[1] = jnp.broadcast_to(-step * alpha, scale.shape[1:])


def correlate_kernel(
    weight, scale, x, z, n, ext_x, ext_z, ext_n, far, extra, kxf, ky, kz, mass, keep, give, total
):
    systems, planes, rows, lanes = z.shape
    slots = systems // 2
    half = slots // 2
    last = planes - 1

    def slot_terms(s, fresh):
        ends = (s, slots + s)
        share = weight[pl.ds(s, 1)]
        on_z = [scale[0, pl.ds(e, 1)] for e in ends]
        on_n = [scale[1, pl.ds(e, 1)] for e in ends]

        def field(p):
            return [x[e, p] + on_z[i] * z[e, p] + on_n[i] * n[e, p] for i, e in enumerate(ends)]

        def outside():
            found = []
            for i, e in enumerate(ends):
                zm = ext_z[1, e]
                if s < half:
                    nm = ext_n[1, e]
                else:
                    nm = outer_slope(zm, extra[s - half + i * half], z[e, last], far, 1)
                found.append(ext_x[1, e] + on_z[i] * zm + on_n[i] * nm)
            return found

        u, v = field(0)
        for p in range(planes):
            u_up, v_up = field(p + 1) if p < last else outside()
            face_x = kxf[p + 1] if p < last else far[1, 0]
            corr = face_x * (u_up - u) * (v_up - v)
            corr = corr + ky[p] * (next_y(u) - u) * (next_y(v) - v)
            corr = corr + kz[p] * (next_z(u) - u) * (next_z(v) - v)
            corr = corr + mass[p] * u * v
            total[p] = share * corr if fresh else total[p] + share * corr
            u, v = u_up, v_up

    for s in range(slots):
        slot_terms(s, s == 0)
    core = lax.rem(lax.axis_index("grp"), 2)
    deep = keep.shape[2]
    for at in range(keep.shape[0]):
        keep[at] = total[:, pl.ds(pl.multiple_of((2 * at + core) * deep, 8), deep)]
        give[at] = total[:, pl.ds(pl.multiple_of((2 * at + 1 - core) * deep, 8), deep)]


def merge_kernel(keep, got, own, to_2, to_1, to_3):
    mine = lax.div(lax.axis_index("grp"), 2)
    for at, out in ((0, own), (1, to_1), (2, to_2), (3, to_3)):
        block = jnp.bitwise_xor(mine, at)
        out[...] = keep[block] + got[block]


def total_kernel(own, one, two, three, out):
    out[...] = (own[...] + one[...]) + (two[...] + three[...])


def local(
    fwd_start, adj_start, adj_rhs, src_cell, group_count, region_label, cut_flag, region_sigma
):
    slots = fwd_start.shape[1]
    systems = 2 * slots
    planes, rows, lanes = region_label.shape
    groups = lax.axis_size("grp")
    tiles = lax.axis_size("tile")
    cells = planes * rows * lanes

    def held(*shape):
        return VMEM(shape, F32)

    def in_hbm(*arrays):
        return [pltpu.with_memory_space_constraint(a, pltpu.HBM) for a in arrays]

    def pinned(*arrays):
        return [pltpu.with_memory_space_constraint(a, pltpu.VMEM) for a in arrays]

    def params(**more):
        return pltpu.CompilerParams(vmem_limit_bytes=LIMIT, **more)

    half = slots // 2
    field = held(systems, planes, rows, lanes)
    plane_set = held(planes, rows, lanes)
    head = held(systems + 3, rows, lanes)
    message = held(systems + 2 * half, rows, lanes)
    HEAD, EDGES, INTERIOR, NEAR, STEPS = 20, 20, 1, 10000, 1

    def cost(scale):
        return pl.CostEstimate(flops=scale * cells, bytes_accessed=scale * cells, transcendentals=0)


    def opposite(value, parity):
        pairs = []
        for g in range(groups):
            by = 1 if g % 2 == parity else -1
            pairs += [(g * tiles + t, g * tiles + t + by) for t in range(tiles) if 0 <= t + by < tiles]
        return lax.ppermute(value, ("grp", "tile"), pairs)

    head_a, head_b = pl.pallas_call(
        head_kernel,
        out_shape=[head, head],
        in_specs=[IN_HBM] * 5,
        out_specs=[IN_VMEM] * 2,
        scratch_shapes=[
            pltpu.SMEM(region_sigma.shape, F32),
            VMEM((4, rows, lanes), jnp.int32),
            VMEM((4, rows, lanes), jnp.int32),
            VMEM((2, 3, rows, lanes), F32),
            pltpu.SemaphoreType.DMA((9,)),
        ],
        compiler_params=params(),
        cost_estimate=cost(HEAD),
        name="head",
    )(*in_hbm(region_sigma, fwd_start, adj_start, region_label, cut_flag))
    near_a = opposite(head_a, 0)
    near_b = opposite(head_b, 1)

    msg_a, msg_b, x, rhs, kxf, ky, kz, dd, inv, mass, kzb, weight = pl.pallas_call(
        edges_kernel,
        out_shape=[
            message, message, field, held(slots, planes, rows, lanes),
            held(planes + 1, rows, lanes),
            plane_set, plane_set, plane_set, plane_set, plane_set, plane_set,
            held(8, lanes),
        ],
        in_specs=[IN_HBM] * 2 + [IN_SMEM] + [IN_HBM] * 5 + [IN_VMEM] * 2,
        out_specs=[IN_VMEM] * 12,
        scratch_shapes=[
            pltpu.SMEM(region_sigma.shape, F32),
            pltpu.SMEM(src_cell.shape, jnp.int32),
            VMEM((planes, rows, lanes), jnp.int32),
            VMEM((planes, rows, lanes), jnp.int32),
            VMEM((planes, rows, lanes), F32),
            VMEM((planes, rows, lanes), F32),
            pltpu.SemaphoreType.DMA((13,)),
        ],
        compiler_params=params(),
        cost_estimate=cost(EDGES),
        name="edges",
    )(
        *in_hbm(region_sigma, src_cell), group_count,
        *in_hbm(fwd_start, adj_start, adj_rhs, region_label, cut_flag),
        *pinned(head_a, head_b),
    )
    got_a = opposite(msg_a, 0)
    got_b = opposite(msg_b, 1)

    z, n, moments, extra = pl.pallas_call(
        interior_kernel,
        out_shape=[field, field, held(systems, 4, 8, 128), held(2 * half, rows, lanes)],
        in_specs=[IN_HBM] + [IN_VMEM] * 8,
        out_specs=[IN_VMEM] * 4,
        scratch_shapes=[pltpu.SMEM(src_cell.shape, jnp.int32), pltpu.SemaphoreType.DMA],
        compiler_params=params(),
        cost_estimate=cost(INTERIOR),
        name="interior",
    )(*in_hbm(src_cell), *pinned(x, rhs, kxf, ky, kz, mass, inv, kzb))

    pair_of = held(2, systems, rows, lanes)
    z, n, part, ext_x, far, moments = pl.pallas_call(
        near_kernel,
        out_shape=[field, field, pair_of, pair_of, held(2, 8, rows, lanes), held(systems, 4, 8, 128)],
        in_specs=[IN_VMEM] * 16,
        out_specs=[IN_VMEM] * 6,
        input_output_aliases={11: 0, 12: 1},
        compiler_params=params(),
        cost_estimate=cost(NEAR),
        name="near",
    )(*pinned(near_a, near_b, head_a, head_b, msg_a, msg_b, kxf, ky, kz, dd, inv, z, n, moments, mass, kzb))

    moments, extra = lax.optimization_barrier((moments, extra))
    late = lax.ppermute(extra, "tile", [(i + 1, i) for i in range(tiles - 1)])

    n, ext_z, ext_n, moments = pl.pallas_call(
        boundary_kernel,
        out_shape=[field, pair_of, pair_of, held(tiles, systems, 128)],
        in_specs=[IN_VMEM] * 13,
        out_specs=[IN_VMEM] * 4,
        input_output_aliases={11: 0},
        scratch_shapes=[VMEM((4, systems, 128), F32)],
        compiler_params=params(),
        name="boundary",
    )(*pinned(got_a, got_b, head_a, head_b, kxf, ky, kz, far, ext_x, part, z, n, moments))

    parts = lax.all_to_all(moments, "tile", 0, 0)

    blocks = held(groups // 2, planes, rows // groups, lanes)
    block = held(planes, rows // groups, lanes)
    scale = pl.pallas_call(
        steps_kernel,
        out_shape=held(2, systems, lanes),
        in_specs=[IN_VMEM],
        out_specs=IN_VMEM,
        compiler_params=params(),
        cost_estimate=cost(STEPS),
        name="steps",
    )(*pinned(parts))
    keep, give = pl.pallas_call(
        correlate_kernel,
        out_shape=[blocks, blocks],
        in_specs=[IN_VMEM] * 14,
        out_specs=[IN_VMEM] * 2,
        scratch_shapes=[VMEM((planes, rows, lanes), F32)],
        compiler_params=params(),
        name="correlate",
    )(*pinned(weight, scale, x, z, n, ext_x, ext_z, ext_n, far, late, kxf, ky, kz, mass))

    def swapped(value, by):
        return lax.ppermute(value, "grp", [(g, g ^ by) for g in range(groups)])

    got = swapped(give, 1)
    own, *sent = pl.pallas_call(
        merge_kernel,
        out_shape=[block] * 4,
        in_specs=[IN_VMEM] * 2,
        out_specs=[IN_VMEM] * 4,
        compiler_params=params(),
        name="merge",
    )(*pinned(keep, got))
    came = [swapped(value, by) for value, by in zip(sent, (4, 2, 6))]
    return pl.pallas_call(
        total_kernel,
        out_shape=jax.ShapeDtypeStruct((planes, rows // groups, lanes), F32),
        in_specs=[IN_VMEM] * 4,
        out_specs=IN_VMEM,
        compiler_params=params(),
        name="total",
    )(*pinned(own, *came))


def solution(mesh):
    in_specs = (
        P("grp", None, "tile", None, None),
        P("grp", None, "tile", None, None),
        P("grp", None, "tile", None, None),
        P("grp", None),
        P("grp"),
        P("tile", None, None),
        P("tile", None, None),
        P(),
    )
    out_specs = P("tile", "grp", None)
    return jax.shard_map(local, mesh=mesh, in_specs=in_specs, out_specs=out_specs, check_vma=False)
```

```python
import functools
import jax
import jax.numpy as jnp
from jax import lax
from jax.experimental import pallas as pl
from jax.experimental.pallas import tpu as pltpu
from jax.sharding import PartitionSpec as P

MASS = 0.05
SOURCE_AMP = 64.0
F32 = jnp.float32
VMEM = pltpu.VMEM
IN_SMEM = pl.BlockSpec(memory_space=pltpu.SMEM)
IN_VMEM = pl.BlockSpec(memory_space=pltpu.VMEM)
IN_HBM = pl.BlockSpec(memory_space=pltpu.HBM)
LIMIT = 24 * 1024 * 1024


def next_y(v):
    return pltpu.roll(v, v.shape[0] - 1, 0)


def prev_y(v):
    return pltpu.roll(v, 1, 0)


def next_z(v):
    return pltpu.roll(v, v.shape[1] - 1, 1)


def prev_z(v):
    return pltpu.roll(v, 1, 1)


def harmonic(left, right):
    return 2.0 * left * right / (left + right)


def harmonic_or_zero(left, right):
    return 2.0 * left * right / jnp.maximum(left + right, 1e-30)


def lateral_faces(sigma, factor, mean):
    rows = lax.broadcasted_iota(jnp.int32, sigma.shape, 0)
    lanes = lax.broadcasted_iota(jnp.int32, sigma.shape, 1)
    face_y = jnp.where(rows < sigma.shape[0] - 1, factor * mean(sigma, next_y(sigma)), 0.0)
    face_z = jnp.where(lanes < sigma.shape[1] - 1, factor * mean(sigma, next_z(sigma)), 0.0)
    return face_y, face_z


def lateral(v, face_y, face_z, back_z):
    flow_y = face_y * (next_y(v) - v)
    along_z = face_z * (next_z(v) - v) + back_z * (prev_z(v) - v)
    return (flow_y - prev_y(flow_y)) + along_z


def upper_lateral(v, face_y, face_z):
    return face_y * next_y(v) + face_z * next_z(v)


def folded(v):
    rows, lanes = v.shape
    v = v.reshape(rows // 8, 8, lanes).sum(0)
    total = v[:, :128]
    for at in range(128, lanes, 128):
        total = total + v[:, at : at + 128]
    return total


def plane_source(src, slot, plane, shape):
    rows, lanes = shape
    planes = 8
    cell = src[0, slot] - (lax.axis_index("tile") * planes + plane) * (rows * lanes)
    at = lax.broadcasted_iota(jnp.int32, shape, 0) * lanes + lax.broadcasted_iota(jnp.int32, shape, 1)
    return jnp.where(at == cell, SOURCE_AMP, 0.0).astype(F32)


def conductivity(table, names):
    value = jnp.full(names.shape, table[0], F32)
    for region in range(1, table.shape[0]):
        value = jnp.where(names == region, table[region], value)
    return value


def cut_factor(flags):
    return 1.0 - 0.5 * flags.astype(F32)


def head_kernel(table_in, fwd, adj, label, cut, msg_a, msg_b, table, lab, flag, shared, sems):
    slots = fwd.shape[1]
    planes = label.shape[0]
    last = planes - 1
    systems = 2 * slots
    core = lax.rem(lax.axis_index("grp"), 2)
    front, back = pl.ds(0, 2), pl.ds(planes - 2, 2)
    copies = [
        pltpu.make_async_copy(table_in, table, sems.at[0]),
        pltpu.make_async_copy(label.at[front], lab.at[pl.ds(0, 2)], sems.at[1]),
        pltpu.make_async_copy(label.at[back], lab.at[pl.ds(2, 2)], sems.at[2]),
        pltpu.make_async_copy(cut.at[front], flag.at[pl.ds(0, 2)], sems.at[3]),
        pltpu.make_async_copy(cut.at[back], flag.at[pl.ds(2, 2)], sems.at[4]),
    ]
    edges = [(msg_a, core == 0), (msg_b, core == 1)]
    for at, (msg, up) in enumerate(edges):
        edge = jnp.where(up, last, 0)
        for half, source in enumerate((fwd, adj)):
            copies.append(
                pltpu.make_async_copy(
                    source.at[0, :, edge], msg.at[pl.ds(half * slots, slots)], sems.at[5 + 2 * at + half]
                )
            )
    for copy in copies:
        copy.start()
    for copy in copies[:5]:
        copy.wait()
    sigma = [conductivity(table, lab[at]) for at in range(4)]
    factor = [cut_factor(flag[at]) for at in range(4)]
    faces = [harmonic(sigma[at], sigma[at + 1]) * factor[at] for at in (0, 2)]
    for side, at in enumerate((0, 3)):
        shared[side, 0] = sigma[at]
        shared[side, 1] = factor[at]
        shared[side, 2] = faces[side]
    for msg, up in edges:
        side = jnp.where(up, 1, 0)
        for at in range(3):
            msg[systems + at] = shared[side, at]
    for copy in copies[5:]:
        copy.wait()


def edges_kernel(
    table_in, src_in, count, fwd, adj, rhs_in, label, cut, head_a, head_b,
    msg_a, msg_b, x, rhs, kxf, ky, kz, dd, inv, mass, kzb, weight,
    table, src, lab, flag, sig, fac, sems,
):
    slots = fwd.shape[1]
    systems = 2 * slots
    planes, rows, lanes = ky.shape
    last = planes - 1
    copies = [
        pltpu.make_async_copy(table_in, table, sems.at[0]),
        pltpu.make_async_copy(src_in, src, sems.at[1]),
        pltpu.make_async_copy(label, lab, sems.at[2]),
        pltpu.make_async_copy(cut, flag, sems.at[3]),
    ]
    spans = (pl.ds(0, 3), pl.ds(planes - 3, 3), pl.ds(3, planes - 6))
    for at, span in enumerate(spans):
        for half, source in enumerate((fwd, adj)):
            into = x.at[pl.ds(half * slots, slots), span]
            copies.append(pltpu.make_async_copy(source.at[0, :, span], into, sems.at[4 + 3 * at + half]))
        copies.append(pltpu.make_async_copy(rhs_in.at[0, :, span], rhs.at[:, span], sems.at[6 + 3 * at]))
    for copy in copies:
        copy.start()
    slot = lax.broadcasted_iota(jnp.int32, weight.shape, 0)
    weight[...] = jnp.where(slot < count[0], -1.0 / slots, 0.0).astype(F32)
    for copy in copies[:4]:
        copy.wait()

    @pl.loop(0, planes)
    def _(p):
        value = conductivity(table, lab[p])
        factor = cut_factor(flag[p])
        sig[p] = value
        fac[p] = factor
        mass[p] = MASS * value
        face_y, face_z = lateral_faces(value, factor, harmonic)
        ky[p] = face_y
        kz[p] = face_z
        kzb[p] = prev_z(face_z)

    kxf[0] = jnp.zeros((rows, lanes), F32)
    kxf[planes] = jnp.zeros((rows, lanes), F32)

    @pl.loop(1, planes)
    def _(p):
        kxf[p] = harmonic(sig[p - 1], sig[p]) * fac[p - 1]

    @pl.loop(0, planes)
    def _(p):
        face_y = ky[p]
        diag = mass[p] + kxf[p] + kxf[p + 1] + face_y + prev_y(face_y) + kz[p] + kzb[p]
        dd[p] = diag
        inv[p] = 1.0 / diag

    for copy in copies[4:10]:
        copy.wait()
    core = lax.rem(lax.axis_index("grp"), 2)
    half = slots // 2
    for msg, up in ((msg_a, core == 0), (msg_b, core == 1)):
        edge, inner, third = jnp.where(up, last, 0), jnp.where(up, last - 1, 1), jnp.where(up, last - 2, 2)
        face, face_next = jnp.where(up, last, 1), jnp.where(up, last - 1, 2)
        lead = jnp.where(up, half, 0)

        def partial(s, right):
            x0 = x[s, edge]
            total = right - mass[edge] * x0 + lateral(x0, ky[edge], kz[edge], kzb[edge])
            msg[s] = total + kxf[face] * (x[s, inner] - x0)

        def onward(at, s, right):
            x1 = x[s, inner]
            total = right - mass[inner] * x1 + lateral(x1, ky[inner], kz[inner], kzb[inner])
            total = total + kxf[face] * (x[s, edge] - x1) + kxf[face_next] * (x[s, third] - x1)
            msg[systems + at] = inv[inner] * total

        @pl.loop(0, slots)
        def _(s):
            partial(s, plane_source(src, s, edge, (rows, lanes)))
            partial(slots + s, rhs[s, edge])

        @pl.loop(0, half)
        def _(s):
            slot = lead + s
            onward(s, slot, plane_source(src, slot, inner, (rows, lanes)))
            onward(half + s, slots + slot, rhs[slot, inner])

    for copy in copies[10:]:
        copy.wait()


def interior_kernel(src_in, x, rs, kxf, ky, kz, mass, inv, kzb, z, n, moments, extra, src, sem):
    systems, planes, rows, lanes = x.shape
    slots = systems // 2
    last = planes - 1
    fetch = pltpu.make_async_copy(src_in, src, sem)
    fetch.start()
    fetch.wait()

    def one(s, right):
        zero = jnp.zeros((8, 128), F32)
        c0, c1, c2, c3 = zero, zero, zero, zero
        for p in range(1, last):
            v = x[s, p]
            total = right(p) - mass[p] * v + lateral(v, ky[p], kz[p], kzb[p])
            total = total + kxf[p + 1] * (x[s, p + 1] - v) + kxf[p] * (x[s, p - 1] - v)
            fresh = inv[p] * total
            z[s, p] = fresh
            c0 = c0 + folded(fresh * total)
        for p in range(1, last):
            v = z[s, p]
            w = mass[p] * v - lateral(v, ky[p], kz[p], kzb[p])
            if p < last - 1:
                w = w - kxf[p + 1] * (z[s, p + 1] - v)
            if p > 1:
                w = w - kxf[p] * (z[s, p - 1] - v)
            if p == 1 or p == last - 1:
                n[s, p] = w
                continue
            m = inv[p] * w
            n[s, p] = m
            c1 = c1 + folded(v * w)
            c2 = c2 + folded(m * w)
            near = upper_lateral(m, ky[p], kz[p])
            if p > 2:
                near = near + kxf[p] * n[s, p - 1]
            c3 = c3 + folded(m * near)
        for at, c in enumerate((c0, c1, c2, c3)):
            moments[s, at] = c

    @pl.loop(0, slots)
    def _(s):
        one(s, lambda p: plane_source(src, s, p, (rows, lanes)))

    @pl.loop(0, slots)
    def _(s):
        one(slots + s, lambda p: rs[s, p])

    half = slots // 2
    for at in range(half):
        extra[at] = z[half + at, 1]
        extra[half + at] = z[slots + half + at, 1]


def both_sides(planes, slots, pairs):
    last, half = planes - 1, slots // 2
    core = lax.rem(lax.axis_index("grp"), 2)
    found = []
    for at, pair in enumerate(pairs):
        low = core == at
        found.append(
            (
                at, pair, low, jnp.where(low, 0, 1),
                jnp.where(low, 0, last), jnp.where(low, 1, last - 1), jnp.where(low, 2, last - 2),
                jnp.where(low, 1, last), jnp.where(low, 2, last - 1), jnp.where(low, half, 0),
            )
        )
    return found


def near_kernel(
    got_a, got_b, head_a, head_b, msg_a, msg_b, kxf, ky, kz, dd, inv, z_in, n_in, moments_in, mass, kzb,
    z, n, part, ext_x, far, moments,
):
    systems, planes, rows, lanes = z.shape
    sides = both_sides(planes, systems // 2, ((got_a, head_b, msg_b), (got_b, head_a, msg_a)))
    for at, (got, head, _), low, side, edge, _, _, _, _, _ in sides:
        sigma, factor, beyond = got[systems], got[systems + 1], got[systems + 2]
        cross = harmonic(sigma, head[systems]) * jnp.where(low, factor, head[systems + 1])
        face_y, face_z = lateral_faces(sigma, factor, harmonic_or_zero)
        there = MASS * sigma + beyond + cross
        back_z = prev_z(face_z)
        there = there + face_y + prev_y(face_y) + face_z + back_z
        real = there > 0.0
        far[side, 0] = cross
        far[side, 1] = jnp.where(real, 1.0 / jnp.where(real, there, 1.0), 0.0)
        far[side, 2] = face_y
        far[side, 3] = face_z
        far[side, 4] = 1.0 / (dd[edge] + cross)
        far[side, 5] = MASS * sigma
        far[side, 6] = beyond
        far[side, 7] = back_z

    @pl.loop(0, systems, unroll=2)
    def _(s):
        c0, c1, c2, c3 = [moments_in[s, at] for at in range(4)]
        for at, (got, head, msg), _, side, edge, inner, third, face, face_next, _ in sides:
            xm = got[s]
            total = msg[s] + far[side, 0] * (xm - head[s])
            z0 = far[side, 4] * total
            z1 = z_in[s, inner]
            flow = kxf[face] * (z1 - z0)
            w0 = mass[edge] * z0 - lateral(z0, ky[edge], kz[edge], kzb[edge]) - flow
            w1 = n_in[s, inner] + flow
            n1 = inv[inner] * w1
            z[s, edge] = z0
            n[s, inner] = n1
            part[side, s] = w0
            ext_x[side, s] = xm
            c0 = c0 + folded(total * z0)
            c1 = c1 + folded(z0 * w0 + z1 * w1)
            c2 = c2 + folded(n1 * w1)
            near = upper_lateral(n1, ky[inner], kz[inner]) + kxf[face_next] * n_in[s, third]
            c3 = c3 + folded(n1 * near)
        for at, c in enumerate((c0, c1, c2, c3)):
            moments[s, at] = c


def moment_lanes(systems):
    lane = lax.broadcasted_iota(jnp.int32, (systems, 128), 1)
    row = lax.broadcasted_iota(jnp.int32, (systems, 128), 0)
    return [lane == 4 * row + at for at in range(4)]


def outer_slope(v, beyond, edge, far, side):
    w = far[side, 5] * v - lateral(v, far[side, 2], far[side, 3], far[side, 7])
    w = w - far[side, 6] * (beyond - v) - far[side, 0] * (edge - v)
    return far[side, 1] * w


def boundary_kernel(
    got_a, got_b, head_a, head_b, kxf, ky, kz, far, ext_x, part, z, n_in, moments,
    n, ext_z, ext_n, out,
    sums,
):
    systems, planes, rows, lanes = n.shape
    slots = systems // 2
    half = slots // 2
    sides = both_sides(planes, slots, ((got_a, head_b), (got_b, head_a)))

    @pl.loop(0, systems, unroll=2)
    def _(s):
        c0, c1, c2, c3 = [moments[s, at] for at in range(4)]
        for _, (got, head), _, side, edge, inner, _, face, _, _ in sides:
            cross = far[side, 0]
            z0 = z[s, edge]
            zm = far[side, 1] * (got[s] + cross * (head[s] - ext_x[side, s]))
            over = cross * (zm - z0)
            w0 = part[side, s] - over
            n0 = far[side, 4] * w0
            n[s, edge] = n0
            ext_z[side, s] = zm
            c1 = c1 - folded(z0 * over)
            c2 = c2 + folded(n0 * w0)
            near = upper_lateral(n0, ky[edge], kz[edge]) + kxf[face] * n_in[s, inner]
            c3 = c3 + folded(n0 * near)
        for at, c in enumerate((c0, c1, c2, c3 + c3)):
            sums[at, pl.ds(s, 1)] = c.sum(0, keepdims=True)

    @pl.loop(0, half, unroll=2)
    def _(at):
        for _, (got, _), _, side, edge, _, _, _, _, lead in sides:
            for place, s in ((at, lead + at), (half + at, slots + lead + at)):
                nm = outer_slope(ext_z[side, s], got[systems + place], z[s, edge], far, side)
                ext_n[side, s] = nm
                pair = folded(far[side, 0] * nm * n[s, edge])
                sums[3, pl.ds(s, 1)] = sums[3, pl.ds(s, 1)] + 2.0 * pair.sum(0, keepdims=True)

    packed = jnp.zeros((systems, 128), F32)
    for at, here in enumerate(moment_lanes(systems)):
        packed = packed + jnp.where(here, sums[at].sum(1, keepdims=True), 0.0)
    out[...] = jnp.broadcast_to(packed.sum(0, keepdims=True)[None], out.shape)


def steps_kernel(parts, scale):
    systems = scale.shape[1]
    summed = jnp.broadcast_to(parts[...].sum(0), (systems, 128))
    m0, m1, m2, c3 = [
        jnp.where(here, summed, 0.0).sum(1, keepdims=True) for here in moment_lanes(systems)
    ]
    unit = 1.0 / m1
    m0, m1, m2, c3 = m0 * unit, m1 * unit, m2 * unit, c3 * unit
    alpha = m0 / m1
    top = m0 * (m2 - m1) + m1 * (m0 - m1)
    low = -m1 * c3 - m2 * (m2 - m1)
    real = jnp.logical_and(top > 0.0, low > 0.0)
    step = jnp.where(real, top * m1 / jnp.where(real, m0 * low, 1.0), 0.0)
    grown = 1.0 + top / (m1 * m1)
    scale[0] = jnp.broadcast_to(alpha + step * grown, scale.shape[1:])
    scale[1] = jnp.broadcast_to(-step * alpha, scale.shape[1:])


def correlate_kernel(
    weight, scale, x, z, n, ext_x, ext_z, ext_n, far, extra, kxf, ky, kz, mass, keep, give, total
):
    systems, planes, rows, lanes = z.shape
    slots = systems // 2
    half = slots // 2
    last = planes - 1

    def slot_terms(s, fresh):
        ends = (s, slots + s)
        share = weight[pl.ds(s, 1)]
        on_z = [scale[0, pl.ds(e, 1)] for e in ends]
        on_n = [scale[1, pl.ds(e, 1)] for e in ends]

        def field(p):
            return [x[e, p] + on_z[i] * z[e, p] + on_n[i] * n[e, p] for i, e in enumerate(ends)]

        def outside():
            found = []
            for i, e in enumerate(ends):
                zm = ext_z[1, e]
                if s < half:
                    nm = ext_n[1, e]
                else:
                    nm = outer_slope(zm, extra[s - half + i * half], z[e, last], far, 1)
                found.append(ext_x[1, e] + on_z[i] * zm + on_n[i] * nm)
            return found

        u, v = field(0)
        for p in range(planes):
            u_up, v_up = field(p + 1) if p < last else outside()
            face_x = kxf[p + 1] if p < last else far[1, 0]
            corr = face_x * (u_up - u) * (v_up - v)
            corr = corr + ky[p] * (next_y(u) - u) * (next_y(v) - v)
            corr = corr + kz[p] * (next_z(u) - u) * (next_z(v) - v)
            corr = corr + mass[p] * u * v
            total[p] = share * corr if fresh else total[p] + share * corr
            u, v = u_up, v_up

    for s in range(slots):
        slot_terms(s, s == 0)
    core = lax.rem(lax.axis_index("grp"), 2)
    deep = keep.shape[2]
    for at in range(keep.shape[0]):
        keep[at] = total[:, pl.ds(pl.multiple_of((2 * at + core) * deep, 8), deep)]
        give[at] = total[:, pl.ds(pl.multiple_of((2 * at + 1 - core) * deep, 8), deep)]


def merge_kernel(keep, got, own, to_2, to_1, to_3):
    mine = lax.div(lax.axis_index("grp"), 2)
    for at, out in ((0, own), (1, to_1), (2, to_2), (3, to_3)):
        block = jnp.bitwise_xor(mine, at)
        out[...] = keep[block] + got[block]


def total_kernel(own, one, two, three, out):
    out[...] = (own[...] + one[...]) + (two[...] + three[...])


def local(
    fwd_start, adj_start, adj_rhs, src_cell, group_count, region_label, cut_flag, region_sigma
):
    slots = fwd_start.shape[1]
    systems = 2 * slots
    planes, rows, lanes = region_label.shape
    groups = lax.axis_size("grp")
    tiles = lax.axis_size("tile")
    cells = planes * rows * lanes

    def held(*shape):
        return VMEM(shape, F32)

    def in_hbm(*arrays):
        return [pltpu.with_memory_space_constraint(a, pltpu.HBM) for a in arrays]

    def pinned(*arrays):
        return [pltpu.with_memory_space_constraint(a, pltpu.VMEM) for a in arrays]

    def params(**more):
        return pltpu.CompilerParams(vmem_limit_bytes=LIMIT, **more)

    half = slots // 2
    field = held(systems, planes, rows, lanes)
    plane_set = held(planes, rows, lanes)
    head = held(systems + 3, rows, lanes)
    message = held(systems + 2 * half, rows, lanes)
    HEAD, EDGES, INTERIOR, NEAR, STEPS = 20, 20, 1, 10000, 1

    def cost(scale):
        return pl.CostEstimate(flops=scale * cells, bytes_accessed=scale * cells, transcendentals=0)


    def opposite(value, parity):
        pairs = []
        for g in range(groups):
            by = 1 if g % 2 == parity else -1
            pairs += [(g * tiles + t, g * tiles + t + by) for t in range(tiles) if 0 <= t + by < tiles]
        return lax.ppermute(value, ("grp", "tile"), pairs)

    head_a, head_b = pl.pallas_call(
        head_kernel,
        out_shape=[head, head],
        in_specs=[IN_HBM] * 5,
        out_specs=[IN_VMEM] * 2,
        scratch_shapes=[
            pltpu.SMEM(region_sigma.shape, F32),
            VMEM((4, rows, lanes), jnp.int32),
            VMEM((4, rows, lanes), jnp.int32),
            VMEM((2, 3, rows, lanes), F32),
            pltpu.SemaphoreType.DMA((9,)),
        ],
        compiler_params=params(),
        cost_estimate=cost(HEAD),
        name="head",
    )(*in_hbm(region_sigma, fwd_start, adj_start, region_label, cut_flag))
    near_a = opposite(head_a, 0)
    near_b = opposite(head_b, 1)

    msg_a, msg_b, x, rhs, kxf, ky, kz, dd, inv, mass, kzb, weight = pl.pallas_call(
        edges_kernel,
        out_shape=[
            message, message, field, held(slots, planes, rows, lanes),
            held(planes + 1, rows, lanes),
            plane_set, plane_set, plane_set, plane_set, plane_set, plane_set,
            held(8, lanes),
        ],
        in_specs=[IN_HBM] * 2 + [IN_SMEM] + [IN_HBM] * 5 + [IN_VMEM] * 2,
        out_specs=[IN_VMEM] * 12,
        scratch_shapes=[
            pltpu.SMEM(region_sigma.shape, F32),
            pltpu.SMEM(src_cell.shape, jnp.int32),
            VMEM((planes, rows, lanes), jnp.int32),
            VMEM((planes, rows, lanes), jnp.int32),
            VMEM((planes, rows, lanes), F32),
            VMEM((planes, rows, lanes), F32),
            pltpu.SemaphoreType.DMA((13,)),
        ],
        compiler_params=params(),
        cost_estimate=cost(EDGES),
        name="edges",
    )(
        *in_hbm(region_sigma, src_cell), group_count,
        *in_hbm(fwd_start, adj_start, adj_rhs, region_label, cut_flag),
        *pinned(head_a, head_b),
    )
    got_a = opposite(msg_a, 0)
    got_b = opposite(msg_b, 1)

    z, n, moments, extra = pl.pallas_call(
        interior_kernel,
        out_shape=[field, field, held(systems, 4, 8, 128), held(2 * half, rows, lanes)],
        in_specs=[IN_HBM] + [IN_VMEM] * 8,
        out_specs=[IN_VMEM] * 4,
        scratch_shapes=[pltpu.SMEM(src_cell.shape, jnp.int32), pltpu.SemaphoreType.DMA],
        compiler_params=params(),
        cost_estimate=cost(INTERIOR),
        name="interior",
    )(*in_hbm(src_cell), *pinned(x, rhs, kxf, ky, kz, mass, inv, kzb))

    pair_of = held(2, systems, rows, lanes)
    z, n, part, ext_x, far, moments = pl.pallas_call(
        near_kernel,
        out_shape=[field, field, pair_of, pair_of, held(2, 8, rows, lanes), held(systems, 4, 8, 128)],
        in_specs=[IN_VMEM] * 16,
        out_specs=[IN_VMEM] * 6,
        input_output_aliases={11: 0, 12: 1},
        compiler_params=params(),
        cost_estimate=cost(NEAR),
        name="near",
    )(*pinned(near_a, near_b, head_a, head_b, msg_a, msg_b, kxf, ky, kz, dd, inv, z, n, moments, mass, kzb))

    moments, extra = lax.optimization_barrier((moments, extra))
    late = lax.ppermute(extra, "tile", [(i + 1, i) for i in range(tiles - 1)])

    n, ext_z, ext_n, moments = pl.pallas_call(
        boundary_kernel,
        out_shape=[field, pair_of, pair_of, held(tiles, 1, 128)],
        in_specs=[IN_VMEM] * 13,
        out_specs=[IN_VMEM] * 4,
        input_output_aliases={11: 0},
        scratch_shapes=[VMEM((4, systems, 128), F32)],
        compiler_params=params(),
        name="boundary",
    )(*pinned(got_a, got_b, head_a, head_b, kxf, ky, kz, far, ext_x, part, z, n, moments))

    parts = lax.all_to_all(moments, "tile", 0, 0)

    blocks = held(groups // 2, planes, rows // groups, lanes)
    block = held(planes, rows // groups, lanes)
    scale = pl.pallas_call(
        steps_kernel,
        out_shape=held(2, systems, lanes),
        in_specs=[IN_VMEM],
        out_specs=IN_VMEM,
        compiler_params=params(),
        cost_estimate=cost(STEPS),
        name="steps",
    )(*pinned(parts))
    keep, give = pl.pallas_call(
        correlate_kernel,
        out_shape=[blocks, blocks],
        in_specs=[IN_VMEM] * 14,
        out_specs=[IN_VMEM] * 2,
        scratch_shapes=[VMEM((planes, rows, lanes), F32)],
        compiler_params=params(),
        name="correlate",
    )(*pinned(weight, scale, x, z, n, ext_x, ext_z, ext_n, far, late, kxf, ky, kz, mass))

    def swapped(value, by):
        return lax.ppermute(value, "grp", [(g, g ^ by) for g in range(groups)])

    got = swapped(give, 1)
    own, *sent = pl.pallas_call(
        merge_kernel,
        out_shape=[block] * 4,
        in_specs=[IN_VMEM] * 2,
        out_specs=[IN_VMEM] * 4,
        compiler_params=params(),
        name="merge",
    )(*pinned(keep, got))
    came = [swapped(value, by) for value, by in zip(sent, (4, 2, 6))]
    return pl.pallas_call(
        total_kernel,
        out_shape=jax.ShapeDtypeStruct((planes, rows // groups, lanes), F32),
        in_specs=[IN_VMEM] * 4,
        out_specs=IN_VMEM,
        compiler_params=params(),
        name="total",
    )(*pinned(own, *came))


def solution(mesh):
    in_specs = (
        P("grp", None, "tile", None, None),
        P("grp", None, "tile", None, None),
        P("grp", None, "tile", None, None),
        P("grp", None),
        P("grp"),
        P("tile", None, None),
        P("tile", None, None),
        P(),
    )
    out_specs = P("tile", "grp", None)
    return jax.shard_map(local, mesh=mesh, in_specs=in_specs, out_specs=out_specs, check_vma=False)
```

```python
import functools
import jax
import jax.numpy as jnp
from jax import lax
from jax.experimental import pallas as pl
from jax.experimental.pallas import tpu as pltpu
from jax.sharding import PartitionSpec as P

MASS = 0.05
SOURCE_AMP = 64.0
F32 = jnp.float32
VMEM = pltpu.VMEM
IN_SMEM = pl.BlockSpec(memory_space=pltpu.SMEM)
IN_VMEM = pl.BlockSpec(memory_space=pltpu.VMEM)
IN_HBM = pl.BlockSpec(memory_space=pltpu.HBM)
LIMIT = 24 * 1024 * 1024


def next_y(v):
    return pltpu.roll(v, v.shape[0] - 1, 0)


def prev_y(v):
    return pltpu.roll(v, 1, 0)


def next_z(v):
    return pltpu.roll(v, v.shape[1] - 1, 1)


def prev_z(v):
    return pltpu.roll(v, 1, 1)


def harmonic(left, right):
    return 2.0 * left * right / (left + right)


def harmonic_or_zero(left, right):
    return 2.0 * left * right / jnp.maximum(left + right, 1e-30)


def lateral_faces(sigma, factor, mean):
    rows = lax.broadcasted_iota(jnp.int32, sigma.shape, 0)
    lanes = lax.broadcasted_iota(jnp.int32, sigma.shape, 1)
    face_y = jnp.where(rows < sigma.shape[0] - 1, factor * mean(sigma, next_y(sigma)), 0.0)
    face_z = jnp.where(lanes < sigma.shape[1] - 1, factor * mean(sigma, next_z(sigma)), 0.0)
    return face_y, face_z


def lateral(v, face_y, face_z, back_z):
    flow_y = face_y * (next_y(v) - v)
    along_z = face_z * (next_z(v) - v) + back_z * (prev_z(v) - v)
    return (flow_y - prev_y(flow_y)) + along_z


def upper_lateral(v, face_y, face_z):
    return face_y * next_y(v) + face_z * next_z(v)


def folded(v):
    rows, lanes = v.shape
    v = v.reshape(rows // 8, 8, lanes).sum(0)
    total = v[:, :128]
    for at in range(128, lanes, 128):
        total = total + v[:, at : at + 128]
    return total


def plane_source(src, slot, plane, shape):
    rows, lanes = shape
    planes = 8
    cell = src[0, slot] - (lax.axis_index("tile") * planes + plane) * (rows * lanes)
    at = lax.broadcasted_iota(jnp.int32, shape, 0) * lanes + lax.broadcasted_iota(jnp.int32, shape, 1)
    return jnp.where(at == cell, SOURCE_AMP, 0.0).astype(F32)


def conductivity(table, names):
    value = jnp.full(names.shape, table[0], F32)
    for region in range(1, table.shape[0]):
        value = jnp.where(names == region, table[region], value)
    return value


def cut_factor(flags):
    return 1.0 - 0.5 * flags.astype(F32)


def head_kernel(table_in, fwd, adj, label, cut, msg_a, msg_b, table, lab, flag, sems):
    slots = fwd.shape[1]
    planes = label.shape[0]
    last = planes - 1
    systems = 2 * slots
    core = lax.rem(lax.axis_index("grp"), 2)
    front, back = pl.ds(0, 2), pl.ds(planes - 2, 2)
    copies = [
        pltpu.make_async_copy(table_in, table, sems.at[0]),
        pltpu.make_async_copy(label.at[front], lab.at[pl.ds(0, 2)], sems.at[1]),
        pltpu.make_async_copy(label.at[back], lab.at[pl.ds(2, 2)], sems.at[2]),
        pltpu.make_async_copy(cut.at[front], flag.at[pl.ds(0, 2)], sems.at[3]),
        pltpu.make_async_copy(cut.at[back], flag.at[pl.ds(2, 2)], sems.at[4]),
    ]
    edges = [(msg_a, core == 0), (msg_b, core == 1)]
    for at, (msg, up) in enumerate(edges):
        edge = jnp.where(up, last, 0)
        for half, source in enumerate((fwd, adj)):
            copies.append(
                pltpu.make_async_copy(
                    source.at[0, :, edge], msg.at[pl.ds(half * slots, slots)], sems.at[5 + 2 * at + half]
                )
            )
    for copy in copies:
        copy.start()
    for copy in copies[:5]:
        copy.wait()
    sigma = [conductivity(table, lab[at]) for at in range(4)]
    factor = [cut_factor(flag[at]) for at in range(4)]
    faces = [harmonic(sigma[at], sigma[at + 1]) * factor[at] for at in (0, 2)]
    for msg, up in edges:
        msg[systems] = jnp.where(up, sigma[3], sigma[0])
        msg[systems + 1] = jnp.where(up, factor[3], factor[0])
        msg[systems + 2] = jnp.where(up, faces[1], faces[0])
    for copy in copies[5:]:
        copy.wait()


def edges_kernel(
    table_in, src_in, count, fwd, adj, rhs_in, label, cut, head_a, head_b,
    msg_a, msg_b, x, rhs, kxf, ky, kz, dd, inv, mass, kzb, weight,
    table, src, lab, flag, sig, fac, sems,
):
    slots = fwd.shape[1]
    systems = 2 * slots
    planes, rows, lanes = ky.shape
    last = planes - 1
    copies = [
        pltpu.make_async_copy(table_in, table, sems.at[0]),
        pltpu.make_async_copy(src_in, src, sems.at[1]),
        pltpu.make_async_copy(label, lab, sems.at[2]),
        pltpu.make_async_copy(cut, flag, sems.at[3]),
    ]
    spans = (pl.ds(0, 3), pl.ds(planes - 3, 3), pl.ds(3, planes - 6))
    for at, span in enumerate(spans):
        for half, source in enumerate((fwd, adj)):
            into = x.at[pl.ds(half * slots, slots), span]
            copies.append(pltpu.make_async_copy(source.at[0, :, span], into, sems.at[4 + 3 * at + half]))
        copies.append(pltpu.make_async_copy(rhs_in.at[0, :, span], rhs.at[:, span], sems.at[6 + 3 * at]))
    for copy in copies:
        copy.start()
    slot = lax.broadcasted_iota(jnp.int32, weight.shape, 0)
    weight[...] = jnp.where(slot < count[0], -1.0 / slots, 0.0).astype(F32)
    for copy in copies[:4]:
        copy.wait()

    @pl.loop(0, planes, unroll=2)
    def _(p):
        value = conductivity(table, lab[p])
        factor = cut_factor(flag[p])
        sig[p] = value
        fac[p] = factor
        mass[p] = MASS * value
        face_y, face_z = lateral_faces(value, factor, harmonic)
        ky[p] = face_y
        kz[p] = face_z
        kzb[p] = prev_z(face_z)

    kxf[0] = jnp.zeros((rows, lanes), F32)
    kxf[planes] = jnp.zeros((rows, lanes), F32)

    @pl.loop(1, planes)
    def _(p):
        kxf[p] = harmonic(sig[p - 1], sig[p]) * fac[p - 1]

    @pl.loop(0, planes, unroll=2)
    def _(p):
        face_y = ky[p]
        diag = mass[p] + kxf[p] + kxf[p + 1] + face_y + prev_y(face_y) + kz[p] + kzb[p]
        dd[p] = diag
        inv[p] = 1.0 / diag

    for copy in copies[4:10]:
        copy.wait()
    core = lax.rem(lax.axis_index("grp"), 2)
    half = slots // 2
    for msg, up in ((msg_a, core == 0), (msg_b, core == 1)):
        edge, inner, third = jnp.where(up, last, 0), jnp.where(up, last - 1, 1), jnp.where(up, last - 2, 2)
        face, face_next = jnp.where(up, last, 1), jnp.where(up, last - 1, 2)
        lead = jnp.where(up, half, 0)

        def partial(s, right):
            x0 = x[s, edge]
            total = right - mass[edge] * x0 + lateral(x0, ky[edge], kz[edge], kzb[edge])
            msg[s] = total + kxf[face] * (x[s, inner] - x0)

        def onward(at, s, right):
            x1 = x[s, inner]
            total = right - mass[inner] * x1 + lateral(x1, ky[inner], kz[inner], kzb[inner])
            total = total + kxf[face] * (x[s, edge] - x1) + kxf[face_next] * (x[s, third] - x1)
            msg[systems + at] = inv[inner] * total

        @pl.loop(0, slots, unroll=2)
        def _(s):
            partial(s, plane_source(src, s, edge, (rows, lanes)))
            partial(slots + s, rhs[s, edge])

        @pl.loop(0, half, unroll=2)
        def _(s):
            slot = lead + s
            onward(s, slot, plane_source(src, slot, inner, (rows, lanes)))
            onward(half + s, slots + slot, rhs[slot, inner])

    for copy in copies[10:]:
        copy.wait()


def interior_kernel(src_in, x, rs, kxf, ky, kz, mass, inv, kzb, z, n, moments, extra, src, sem):
    systems, planes, rows, lanes = x.shape
    slots = systems // 2
    last = planes - 1
    fetch = pltpu.make_async_copy(src_in, src, sem)
    fetch.start()
    fetch.wait()

    def one(s, right):
        zero = jnp.zeros((8, 128), F32)
        c0, c1, c2, c3 = zero, zero, zero, zero
        for p in range(1, last):
            v = x[s, p]
            total = right(p) - mass[p] * v + lateral(v, ky[p], kz[p], kzb[p])
            total = total + kxf[p + 1] * (x[s, p + 1] - v) + kxf[p] * (x[s, p - 1] - v)
            fresh = inv[p] * total
            z[s, p] = fresh
            c0 = c0 + folded(fresh * total)
        for p in range(1, last):
            v = z[s, p]
            w = mass[p] * v - lateral(v, ky[p], kz[p], kzb[p])
            if p < last - 1:
                w = w - kxf[p + 1] * (z[s, p + 1] - v)
            if p > 1:
                w = w - kxf[p] * (z[s, p - 1] - v)
            if p == 1 or p == last - 1:
                n[s, p] = w
                continue
            m = inv[p] * w
            n[s, p] = m
            c1 = c1 + folded(v * w)
            c2 = c2 + folded(m * w)
            near = upper_lateral(m, ky[p], kz[p])
            if p > 2:
                near = near + kxf[p] * n[s, p - 1]
            c3 = c3 + folded(m * near)
        for at, c in enumerate((c0, c1, c2, c3)):
            moments[s, at] = c

    @pl.loop(0, slots)
    def _(s):
        one(s, lambda p: plane_source(src, s, p, (rows, lanes)))

    @pl.loop(0, slots)
    def _(s):
        one(slots + s, lambda p: rs[s, p])

    half = slots // 2
    for at in range(half):
        extra[at] = z[half + at, 1]
        extra[half + at] = z[slots + half + at, 1]


def both_sides(planes, slots, pairs):
    last, half = planes - 1, slots // 2
    core = lax.rem(lax.axis_index("grp"), 2)
    found = []
    for at, pair in enumerate(pairs):
        low = core == at
        found.append(
            (
                at, pair, low, jnp.where(low, 0, 1),
                jnp.where(low, 0, last), jnp.where(low, 1, last - 1), jnp.where(low, 2, last - 2),
                jnp.where(low, 1, last), jnp.where(low, 2, last - 1), jnp.where(low, half, 0),
            )
        )
    return found


def near_kernel(
    got_a, got_b, head_a, head_b, msg_a, msg_b, kxf, ky, kz, dd, inv, z_in, n_in, moments_in, mass, kzb,
    z, n, part, ext_x, far, moments,
):
    systems, planes, rows, lanes = z.shape
    sides = both_sides(planes, systems // 2, ((got_a, head_b, msg_b), (got_b, head_a, msg_a)))
    for at, (got, head, _), low, side, edge, _, _, _, _, _ in sides:
        sigma, factor, beyond = got[systems], got[systems + 1], got[systems + 2]
        cross = harmonic(sigma, head[systems]) * jnp.where(low, factor, head[systems + 1])
        face_y, face_z = lateral_faces(sigma, factor, harmonic_or_zero)
        there = MASS * sigma + beyond + cross
        back_z = prev_z(face_z)
        there = there + face_y + prev_y(face_y) + face_z + back_z
        real = there > 0.0
        far[side, 0] = cross
        far[side, 1] = jnp.where(real, 1.0 / jnp.where(real, there, 1.0), 0.0)
        far[side, 2] = face_y
        far[side, 3] = face_z
        far[side, 4] = 1.0 / (dd[edge] + cross)
        far[side, 5] = MASS * sigma
        far[side, 6] = beyond
        far[side, 7] = back_z

    @pl.loop(0, systems, unroll=4)
    def _(s):
        c0, c1, c2, c3 = [moments_in[s, at] for at in range(4)]
        for at, (got, head, msg), _, side, edge, inner, third, face, face_next, _ in sides:
            xm = got[s]
            total = msg[s] + far[side, 0] * (xm - head[s])
            z0 = far[side, 4] * total
            z1 = z_in[s, inner]
            flow = kxf[face] * (z1 - z0)
            w0 = mass[edge] * z0 - lateral(z0, ky[edge], kz[edge], kzb[edge]) - flow
            w1 = n_in[s, inner] + flow
            n1 = inv[inner] * w1
            z[s, edge] = z0
            n[s, inner] = n1
            part[side, s] = w0
            ext_x[side, s] = xm
            c0 = c0 + folded(total * z0)
            c1 = c1 + folded(z0 * w0 + z1 * w1)
            c2 = c2 + folded(n1 * w1)
            near = upper_lateral(n1, ky[inner], kz[inner]) + kxf[face_next] * n_in[s, third]
            c3 = c3 + folded(n1 * near)
        for at, c in enumerate((c0, c1, c2, c3)):
            moments[s, at] = c


def moment_lanes(systems):
    lane = lax.broadcasted_iota(jnp.int32, (systems, 128), 1)
    row = lax.broadcasted_iota(jnp.int32, (systems, 128), 0)
    return [lane == 4 * row + at for at in range(4)]


def outer_slope(v, beyond, edge, far, side):
    w = far[side, 5] * v - lateral(v, far[side, 2], far[side, 3], far[side, 7])
    w = w - far[side, 6] * (beyond - v) - far[side, 0] * (edge - v)
    return far[side, 1] * w


def boundary_kernel(
    got_a, got_b, head_a, head_b, kxf, ky, kz, far, ext_x, part, z, n_in, moments,
    n, ext_z, ext_n, out,
    sums,
):
    systems, planes, rows, lanes = n.shape
    slots = systems // 2
    half = slots // 2
    sides = both_sides(planes, slots, ((got_a, head_b), (got_b, head_a)))

    @pl.loop(0, systems, unroll=4)
    def _(s):
        c0, c1, c2, c3 = [moments[s, at] for at in range(4)]
        for _, (got, head), _, side, edge, inner, _, face, _, _ in sides:
            cross = far[side, 0]
            z0 = z[s, edge]
            zm = far[side, 1] * (got[s] + cross * (head[s] - ext_x[side, s]))
            over = cross * (zm - z0)
            w0 = part[side, s] - over
            n0 = far[side, 4] * w0
            n[s, edge] = n0
            ext_z[side, s] = zm
            c1 = c1 - folded(z0 * over)
            c2 = c2 + folded(n0 * w0)
            near = upper_lateral(n0, ky[edge], kz[edge]) + kxf[face] * n_in[s, inner]
            c3 = c3 + folded(n0 * near)
        for at, c in enumerate((c0, c1, c2, c3 + c3)):
            sums[at, pl.ds(s, 1)] = c.sum(0, keepdims=True)

    @pl.loop(0, half, unroll=2)
    def _(at):
        for _, (got, _), _, side, edge, _, _, _, _, lead in sides:
            for place, s in ((at, lead + at), (half + at, slots + lead + at)):
                nm = outer_slope(ext_z[side, s], got[systems + place], z[s, edge], far, side)
                ext_n[side, s] = nm
                pair = folded(far[side, 0] * nm * n[s, edge])
                sums[3, pl.ds(s, 1)] = sums[3, pl.ds(s, 1)] + 2.0 * pair.sum(0, keepdims=True)

    packed = jnp.zeros((systems, 128), F32)
    for at, here in enumerate(moment_lanes(systems)):
        packed = packed + jnp.where(here, sums[at].sum(1, keepdims=True), 0.0)
    out[...] = jnp.broadcast_to(packed.sum(0, keepdims=True)[None], out.shape)


def steps_kernel(parts, scale):
    systems = scale.shape[1]
    summed = jnp.broadcast_to(parts[...].sum(0), (systems, 128))
    m0, m1, m2, c3 = [
        jnp.where(here, summed, 0.0).sum(1, keepdims=True) for here in moment_lanes(systems)
    ]
    unit = 1.0 / m1
    m0, m1, m2, c3 = m0 * unit, m1 * unit, m2 * unit, c3 * unit
    alpha = m0 / m1
    top = m0 * (m2 - m1) + m1 * (m0 - m1)
    low = -m1 * c3 - m2 * (m2 - m1)
    real = jnp.logical_and(top > 0.0, low > 0.0)
    step = jnp.where(real, top * m1 / jnp.where(real, m0 * low, 1.0), 0.0)
    grown = 1.0 + top / (m1 * m1)
    scale[0] = jnp.broadcast_to(alpha + step * grown, scale.shape[1:])
    scale[1] = jnp.broadcast_to(-step * alpha, scale.shape[1:])


def correlate_kernel(
    weight, scale, x, z, n, ext_x, ext_z, ext_n, far, extra, kxf, ky, kz, mass, keep, give, total
):
    systems, planes, rows, lanes = z.shape
    slots = systems // 2
    half = slots // 2
    last = planes - 1

    def slot_terms(s, fresh):
        ends = (s, slots + s)
        share = weight[pl.ds(s, 1)]
        on_z = [scale[0, pl.ds(e, 1)] for e in ends]
        on_n = [scale[1, pl.ds(e, 1)] for e in ends]

        def field(p):
            return [x[e, p] + on_z[i] * z[e, p] + on_n[i] * n[e, p] for i, e in enumerate(ends)]

        def outside():
            found = []
            for i, e in enumerate(ends):
                zm = ext_z[1, e]
                if s < half:
                    nm = ext_n[1, e]
                else:
                    nm = outer_slope(zm, extra[s - half + i * half], z[e, last], far, 1)
                found.append(ext_x[1, e] + on_z[i] * zm + on_n[i] * nm)
            return found

        u, v = field(0)
        for p in range(planes):
            u_up, v_up = field(p + 1) if p < last else outside()
            face_x = kxf[p + 1] if p < last else far[1, 0]
            corr = face_x * (u_up - u) * (v_up - v)
            corr = corr + ky[p] * (next_y(u) - u) * (next_y(v) - v)
            corr = corr + kz[p] * (next_z(u) - u) * (next_z(v) - v)
            corr = corr + mass[p] * u * v
            total[p] = share * corr if fresh else total[p] + share * corr
            u, v = u_up, v_up

    for s in range(slots):
        slot_terms(s, s == 0)
    core = lax.rem(lax.axis_index("grp"), 2)
    deep = keep.shape[2]
    for at in range(keep.shape[0]):
        keep[at] = total[:, pl.ds(pl.multiple_of((2 * at + core) * deep, 8), deep)]
        give[at] = total[:, pl.ds(pl.multiple_of((2 * at + 1 - core) * deep, 8), deep)]


def merge_kernel(keep, got, own, to_2, to_1, to_3):
    mine = lax.div(lax.axis_index("grp"), 2)
    for at, out in ((0, own), (1, to_1), (2, to_2), (3, to_3)):
        block = jnp.bitwise_xor(mine, at)
        out[...] = keep[block] + got[block]


def total_kernel(own, one, two, three, out):
    out[...] = (own[...] + one[...]) + (two[...] + three[...])


def local(
    fwd_start, adj_start, adj_rhs, src_cell, group_count, region_label, cut_flag, region_sigma
):
    slots = fwd_start.shape[1]
    systems = 2 * slots
    planes, rows, lanes = region_label.shape
    groups = lax.axis_size("grp")
    tiles = lax.axis_size("tile")
    cells = planes * rows * lanes

    def held(*shape):
        return VMEM(shape, F32)

    def in_hbm(*arrays):
        return [pltpu.with_memory_space_constraint(a, pltpu.HBM) for a in arrays]

    def pinned(*arrays):
        return [pltpu.with_memory_space_constraint(a, pltpu.VMEM) for a in arrays]

    def params(**more):
        return pltpu.CompilerParams(vmem_limit_bytes=LIMIT, **more)

    half = slots // 2
    field = held(systems, planes, rows, lanes)
    plane_set = held(planes, rows, lanes)
    head = held(systems + 3, rows, lanes)
    message = held(systems + 2 * half, rows, lanes)
    HEAD, EDGES, INTERIOR, NEAR, STEPS = 20, 20, 1, 10000, 1

    def cost(scale):
        return pl.CostEstimate(flops=scale * cells, bytes_accessed=scale * cells, transcendentals=0)


    def opposite(value, parity):
        pairs = []
        for g in range(groups):
            by = 1 if g % 2 == parity else -1
            pairs += [(g * tiles + t, g * tiles + t + by) for t in range(tiles) if 0 <= t + by < tiles]
        return lax.ppermute(value, ("grp", "tile"), pairs)

    head_a, head_b = pl.pallas_call(
        head_kernel,
        out_shape=[head, head],
        in_specs=[IN_HBM] * 5,
        out_specs=[IN_VMEM] * 2,
        scratch_shapes=[
            pltpu.SMEM(region_sigma.shape, F32),
            VMEM((4, rows, lanes), jnp.int32),
            VMEM((4, rows, lanes), jnp.int32),
            pltpu.SemaphoreType.DMA((9,)),
        ],
        compiler_params=params(),
        cost_estimate=cost(HEAD),
        name="head",
    )(*in_hbm(region_sigma, fwd_start, adj_start, region_label, cut_flag))
    near_a = opposite(head_a, 0)
    near_b = opposite(head_b, 1)

    msg_a, msg_b, x, rhs, kxf, ky, kz, dd, inv, mass, kzb, weight = pl.pallas_call(
        edges_kernel,
        out_shape=[
            message, message, field, held(slots, planes, rows, lanes),
            held(planes + 1, rows, lanes),
            plane_set, plane_set, plane_set, plane_set, plane_set, plane_set,
            held(8, lanes),
        ],
        in_specs=[IN_HBM] * 2 + [IN_SMEM] + [IN_HBM] * 5 + [IN_VMEM] * 2,
        out_specs=[IN_VMEM] * 12,
        scratch_shapes=[
            pltpu.SMEM(region_sigma.shape, F32),
            pltpu.SMEM(src_cell.shape, jnp.int32),
            VMEM((planes, rows, lanes), jnp.int32),
            VMEM((planes, rows, lanes), jnp.int32),
            VMEM((planes, rows, lanes), F32),
            VMEM((planes, rows, lanes), F32),
            pltpu.SemaphoreType.DMA((13,)),
        ],
        compiler_params=params(),
        cost_estimate=cost(EDGES),
        name="edges",
    )(
        *in_hbm(region_sigma, src_cell), group_count,
        *in_hbm(fwd_start, adj_start, adj_rhs, region_label, cut_flag),
        *pinned(head_a, head_b),
    )
    got_a = opposite(msg_a, 0)
    got_b = opposite(msg_b, 1)

    z, n, moments, extra = pl.pallas_call(
        interior_kernel,
        out_shape=[field, field, held(systems, 4, 8, 128), held(2 * half, rows, lanes)],
        in_specs=[IN_HBM] + [IN_VMEM] * 8,
        out_specs=[IN_VMEM] * 4,
        scratch_shapes=[pltpu.SMEM(src_cell.shape, jnp.int32), pltpu.SemaphoreType.DMA],
        compiler_params=params(),
        cost_estimate=cost(INTERIOR),
        name="interior",
    )(*in_hbm(src_cell), *pinned(x, rhs, kxf, ky, kz, mass, inv, kzb))

    pair_of = held(2, systems, rows, lanes)
    z, n, part, ext_x, far, moments = pl.pallas_call(
        near_kernel,
        out_shape=[field, field, pair_of, pair_of, held(2, 8, rows, lanes), held(systems, 4, 8, 128)],
        in_specs=[IN_VMEM] * 16,
        out_specs=[IN_VMEM] * 6,
        input_output_aliases={11: 0, 12: 1},
        compiler_params=params(),
        cost_estimate=cost(NEAR),
        name="near",
    )(*pinned(near_a, near_b, head_a, head_b, msg_a, msg_b, kxf, ky, kz, dd, inv, z, n, moments, mass, kzb))

    moments, extra = lax.optimization_barrier((moments, extra))
    late = lax.ppermute(extra, "tile", [(i + 1, i) for i in range(tiles - 1)])

    n, ext_z, ext_n, moments = pl.pallas_call(
        boundary_kernel,
        out_shape=[field, pair_of, pair_of, held(tiles, 1, 128)],
        in_specs=[IN_VMEM] * 13,
        out_specs=[IN_VMEM] * 4,
        input_output_aliases={11: 0},
        scratch_shapes=[VMEM((4, systems, 128), F32)],
        compiler_params=params(),
        name="boundary",
    )(*pinned(got_a, got_b, head_a, head_b, kxf, ky, kz, far, ext_x, part, z, n, moments))

    parts = lax.all_to_all(moments, "tile", 0, 0)

    blocks = held(groups // 2, planes, rows // groups, lanes)
    block = held(planes, rows // groups, lanes)
    scale = pl.pallas_call(
        steps_kernel,
        out_shape=held(2, systems, lanes),
        in_specs=[IN_VMEM],
        out_specs=IN_VMEM,
        compiler_params=params(),
        cost_estimate=cost(STEPS),
        name="steps",
    )(*pinned(parts))
    keep, give = pl.pallas_call(
        correlate_kernel,
        out_shape=[blocks, blocks],
        in_specs=[IN_VMEM] * 14,
        out_specs=[IN_VMEM] * 2,
        scratch_shapes=[VMEM((planes, rows, lanes), F32)],
        compiler_params=params(),
        name="correlate",
    )(*pinned(weight, scale, x, z, n, ext_x, ext_z, ext_n, far, late, kxf, ky, kz, mass))

    def swapped(value, by):
        return lax.ppermute(value, "grp", [(g, g ^ by) for g in range(groups)])

    got = swapped(give, 1)
    own, *sent = pl.pallas_call(
        merge_kernel,
        out_shape=[block] * 4,
        in_specs=[IN_VMEM] * 2,
        out_specs=[IN_VMEM] * 4,
        compiler_params=params(),
        name="merge",
    )(*pinned(keep, got))
    came = [swapped(value, by) for value, by in zip(sent, (4, 2, 6))]
    return pl.pallas_call(
        total_kernel,
        out_shape=jax.ShapeDtypeStruct((planes, rows // groups, lanes), F32),
        in_specs=[IN_VMEM] * 4,
        out_specs=IN_VMEM,
        compiler_params=params(),
        name="total",
    )(*pinned(own, *came))


def solution(mesh):
    in_specs = (
        P("grp", None, "tile", None, None),
        P("grp", None, "tile", None, None),
        P("grp", None, "tile", None, None),
        P("grp", None),
        P("grp"),
        P("tile", None, None),
        P("tile", None, None),
        P(),
    )
    out_specs = P("tile", "grp", None)
    return jax.shard_map(local, mesh=mesh, in_specs=in_specs, out_specs=out_specs, check_vma=False)
```
